256 devices in a mesh: slab: 16 (over y, x), expert: 16 (over z, core).
Axes of the slice: x: 4, y: 4, z: 8, core: 2. Of those that a mesh axis runs over, the one named last changes fastest.
Arguments:
- features: bfloat16 [32, 32, 128, 128], P(None, 'slab', 'expert'), may hold values from -6 to 6
- kernel: bfloat16 [27, 32, 32], replicated, may hold values from -0.21875 to 0.21875
- labels: int32 [32, 128, 128], P('slab', 'expert'), may hold values from 0 to 116
- region_ids: int32 [16, 16, 16, 1], P('slab', 'expert'), may hold values from 0 to 15; in each aligned block of 16 rows (0 to 15, 16 to 31, ..., all dimensions but the last counted through in order) at most 2 rows name the same one
- first_weight: bfloat16 [16, 256, 32], P('expert'), may hold values from -1 to 1
- first_bias: bfloat16 [16, 256], P('expert'), may hold values from -3 to 3
- second_weight: bfloat16 [16, 117, 256], P('expert'), may hold values from -0.375 to 0.375
- second_bias: bfloat16 [16, 117], P('expert'), may hold values from -3 to 3
Outputs:
- loss: float32 [], replicated
- grad_kernel: float32 [27, 32, 32], replicated
- grad_first_weight: float32 [16, 256, 32], P('expert')
- grad_first_bias: float32 [16, 256], P('expert')
- grad_second_weight: float32 [16, 117, 256], P('expert')
- grad_second_bias: float32 [16, 117], P('expert')
The draws below stay inside these ranges and needn't reach their ends.
Inputs may be any that keep to these rules, and one draw needn't show every extreme that they name: `region_ids`: within the rows of one device no expert is named by more than 2 rows, and in some device one expert is named by exactly 2 rows.
All inputs are finite; a program needn't handle non-finite values.
Results may differ from the reference program's by a relative error of at most 0.013.
Values may be sent and summed in bfloat16 or wider, within the bound.
A program may use at most 64 MiB of HBM per device.

```python
import math
import jax
import jax.numpy as jnp
import numpy as np
from jax import lax

C = 32
HIDDEN_SIZE = 256
NCLS = 117
W = 128
ZDEV = 2
HDEV = 8
ROWS_DEV = 16
CAP = 2
EXP = 16
NZ = 32
NH = 128
N_SLAB = 16
N_EXPERT = 16


def set_ends(entries, own_key, low, top_value):
    spot = [jax.random.randint(jax.random.fold_in(own_key, axis), (), 0, length) for axis, length in enumerate(entries.shape)]
    longest = entries.shape.index(max(entries.shape))
    next_to = spot[:longest] + [(spot[longest] + 1) % entries.shape[longest]] + spot[longest + 1:]
    return entries.at[tuple(spot)].set(low).at[tuple(next_to)].set(top_value)


def levels(key, dims, split, smallest, high):
    gain, own = 1.0, jax.random.fold_in(key, 6)
    for position, shards_of in split:
        heights = jnp.exp(jax.random.uniform(jax.random.fold_in(own, position), (shards_of,), jnp.float32, smallest / len(split), high / len(split)))
        gain = gain * jnp.repeat(heights, dims[position] // shards_of).reshape([-1 if axis == position else 1 for axis in range(len(dims))])
    return gain


def shared_out(key, own, number, rows, amount, top, bound, lean):
    ranking = jax.random.permutation(key, amount)
    heavy_load, ordinary = shares(amount, rows * top, bound, lean, True), shares(amount, rows * top, bound, lean, False)
    places = jnp.arange(amount)

    def named(lengths, rotation):
        used = int((lengths > 0).sum())
        fixed = max(1, used // 4)
        passed = fixed + (places - fixed + rotation * (used - fixed)) % max(1, amount - fixed)
        return jnp.zeros((amount,), jnp.int32).at[ranking[jnp.where(places < fixed, places, passed)]].set(jnp.asarray(lengths, jnp.int32))

    lengths = jnp.where(number % 4 == 0, named(heavy_load, number // 4), named(ordinary, number - number // 4 - 1))
    mixed = jax.random.permutation(jax.random.fold_in(own, 3), amount)
    source_of, sink = mixed[0:amount // 2 * 2:2], mixed[1:amount // 2 * 2:2]
    room = jnp.minimum(lengths[source_of] - 1, bound - lengths[sink]) // 2
    room = jnp.where((source_of == ranking[0]) | (sink == ranking[0]) | (lengths[sink] == 0), 0, jnp.maximum(room, 0))
    passed = jax.random.randint(jax.random.fold_in(own, 4), (amount // 2,), 0, 1 << 20) % (room + 1)
    lengths = lengths.at[source_of].add(-passed).at[sink].add(passed)
    members = jnp.searchsorted(jnp.cumsum(lengths), jnp.arange(rows * top), side="right").astype(jnp.int32)
    listing = members.reshape(top, rows).T
    listing = listing[jax.random.permutation(jax.random.fold_in(own, 1), rows)]
    rotation = jax.random.randint(jax.random.fold_in(own, 2), (rows, 1), 0, top)
    return jnp.take_along_axis(listing, (jnp.arange(top)[None, :] + rotation) % top, axis=1)


def shares(count, total, limit, lean, full):
    weights = [(1 << 20) // math.isqrt(standing ** lean) + 1 for standing in range(1, count + 1)]
    largest = limit if full else min(limit, max(-(-total // count), total * weights[0] // sum(weights)))
    least = 1 if total - largest >= count - 1 else 0
    counts, spare = [largest] + [least] * (count - 1), total - largest - least * (count - 1)
    while spare > 0:
        free = [i for i in range(1, count) if counts[i] < largest] or [i for i in range(1, count) if counts[i] < limit]
        whole, remaining = sum([weights[i] for i in free]), spare
        for i in free:
            extra = min(limit - counts[i], max(1, remaining * weights[i] // whole), spare)
            counts[i] = counts[i] + extra
            spare = spare - extra
    return np.array(counts)


def bell_draw(stream_key, shape, scale, reach, cuts=(), dtype=jnp.bfloat16):
    drawn = jax.random.normal(stream_key, shape, jnp.float32) * scale
    if len(cuts) > 0:
        drawn = levels(stream_key, shape, cuts, -0.22, 0.18) * drawn
    return jnp.clip(drawn, min=-reach, max=reach).astype(dtype)


def setup_inputs(seed: int = 0) -> dict:
    streams_of = jax.random.split(jax.random.key(seed), 9)
    features = bell_draw(streams_of[0], (C, NZ, NH, W), 1.0, 6.0, ((1, 16), (2, 16)))
    kernel = bell_draw(streams_of[1], (27, C, C), (27 * C) ** -0.5, 0.21875)
    labels = set_ends(jax.random.randint(streams_of[2], (NZ, NH, W), 0, NCLS), jax.random.fold_in(streams_of[2], 1), 0, NCLS - 1).astype(jnp.int32)
    region_ids_keys = jax.random.split(jax.random.fold_in(streams_of[3], 1), N_SLAB * N_EXPERT * ROWS_DEV // ROWS_DEV)
    region_ids_turns = jax.random.permutation(jax.random.fold_in(streams_of[3], 3), N_SLAB * N_EXPERT * ROWS_DEV // ROWS_DEV)
    region_ids = jax.vmap(lambda own, number: shared_out(jax.random.fold_in(streams_of[3], 2), own, number, ROWS_DEV, EXP, 1, CAP, 2))(region_ids_keys, region_ids_turns).reshape((N_SLAB, N_EXPERT, ROWS_DEV, 1))
    first_weight = bell_draw(streams_of[4], (EXP, HIDDEN_SIZE, C), C ** -0.5, 1.0, ((0, 16),))
    first_bias = bell_draw(streams_of[5], (EXP, HIDDEN_SIZE), 0.5, 3.0, ((0, 16),))
    second_weight = bell_draw(streams_of[6], (EXP, NCLS, HIDDEN_SIZE), HIDDEN_SIZE ** -0.5, 0.375, ((0, 16),))
    second_bias = bell_draw(streams_of[7], (EXP, NCLS), 0.5, 3.0, ((0, 16),))
    return dict(features=features, kernel=kernel, labels=labels, region_ids=region_ids, first_weight=first_weight, first_bias=first_bias, second_weight=second_weight, second_bias=second_bias)


def silu_grad(pre_value):
    sigmoid_value = jax.nn.sigmoid(pre_value)
    return sigmoid_value * (1.0 + pre_value * (1.0 - sigmoid_value))

def shifted(padded, tap_index, depth_cells, height_cells, width_cells):
    offset_z = tap_index // 9
    offset_h = tap_index % 9 // 3
    offset_w = tap_index % 3
    return padded[:, offset_z:offset_z + depth_cells, offset_h:offset_h + height_cells, offset_w:offset_w + width_cells]

def expert_forward(inputs, weight_one, bias_one, weight_two, bias_two):
    hidden_pre = jnp.einsum('bhc,bcn->bhn', weight_one.astype(jnp.float32), inputs.astype(jnp.float32), precision=lax.Precision.HIGHEST) + bias_one.astype(jnp.float32)[:, :, None]
    hidden_act = jax.nn.silu(hidden_pre).astype(jnp.bfloat16)
    logits = jnp.einsum('bkh,bhn->bkn', weight_two.astype(jnp.float32), hidden_act.astype(jnp.float32), precision=lax.Precision.HIGHEST) + bias_two.astype(jnp.float32)[:, :, None]
    return (hidden_pre, hidden_act, logits.astype(jnp.bfloat16))

def class_sums(logits, labels_block):
    probs = jax.nn.sigmoid(logits.astype(jnp.float32))
    classes = lax.broadcasted_iota(jnp.int32, (1, logits.shape[1], 1), 1)
    onehot = (labels_block[:, None, :] == classes).astype(jnp.float32)
    live = (labels_block >= 0).astype(jnp.float32)[:, None, :]
    return jnp.stack([lax.optimization_barrier(jnp.sum(probs * onehot, axis=(0, 2))), lax.optimization_barrier(jnp.sum(probs * live, axis=(0, 2))), lax.optimization_barrier(jnp.sum(onehot, axis=(0, 2)))])

def expert_backward(inputs, labels_block, weights, totals, loss_scale):
    weight_one, bias_one, weight_two, bias_two = weights
    hidden_pre, hidden_act, logits = expert_forward(inputs, weight_one, bias_one, weight_two, bias_two)
    num_classes = logits.shape[1]
    probs = jax.nn.sigmoid(logits.astype(jnp.float32))
    classes = lax.broadcasted_iota(jnp.int32, (1, num_classes, 1), 1)
    onehot = (labels_block[:, None, :] == classes).astype(jnp.float32)
    live = (labels_block >= 0).astype(jnp.float32)[:, None, :]
    denom = (totals[1] + totals[2] + 1.0)[None, :, None]
    dice = (2.0 * totals[0] + 1.0)[None, :, None] / denom
    grad_prob = -loss_scale / num_classes * (2.0 * onehot - dice) / denom * live
    grad_logit = (grad_prob * probs * (1.0 - probs)).astype(jnp.bfloat16)
    grad_logit_f = grad_logit.astype(jnp.float32)
    grad_two = jnp.einsum('bkn,bhn->bkh', grad_logit_f, hidden_act.astype(jnp.float32), precision=lax.Precision.HIGHEST)
    grad_bias_two = lax.optimization_barrier(jnp.sum(grad_logit_f, axis=2))
    grad_hidden = jnp.einsum('bkh,bkn->bhn', weight_two.astype(jnp.float32), grad_logit_f, precision=lax.Precision.HIGHEST) * silu_grad(hidden_pre)
    grad_hidden = grad_hidden.astype(jnp.bfloat16).astype(jnp.float32)
    grad_one = jnp.einsum('bhn,bcn->bhc', grad_hidden, inputs.astype(jnp.float32), precision=lax.Precision.HIGHEST)
    grad_bias_one = lax.optimization_barrier(jnp.sum(grad_hidden, axis=2))
    grad_inputs = jnp.einsum('bhc,bhn->bcn', weight_one.astype(jnp.float32), grad_hidden, precision=lax.Precision.HIGHEST).astype(jnp.bfloat16)
    return (grad_inputs, (grad_one, grad_bias_one, grad_two, grad_bias_two))

def reference(features, kernel, labels, region_ids, first_weight, first_bias, second_weight, second_bias):
    padded = jnp.pad(features, ((0, 0), (1, 1), (1, 1), (1, 1))).astype(jnp.float32)
    kernel_f = kernel.astype(jnp.float32)
    conv_pre = jnp.zeros((C, NZ, NH, W), jnp.float32)
    for tap_index in range(27):
        conv_pre = conv_pre + jnp.einsum('oc,czhw->ozhw', kernel_f[tap_index], shifted(padded, tap_index, NZ, NH, W), precision=lax.Precision.HIGHEST)
    conv_act = jax.nn.silu(conv_pre).astype(jnp.bfloat16)
    block_rows = 64
    block_count = NZ * NH // block_rows
    row_inputs = jnp.transpose(conv_act, (1, 2, 0, 3)).reshape(block_count, block_rows, C, W)
    id_grid = region_ids.reshape(N_SLAB, N_EXPERT, ZDEV, HDEV).transpose(0, 2, 1, 3).reshape(block_count, block_rows).astype(jnp.int32)
    row_labels = labels.reshape(block_count, block_rows, W)
    loss_scale = 16.0 * NCLS * math.sqrt(NZ * NH * W)

    def first_pass(totals, pieces):
        inputs, ids_block, labels_block = pieces
        logits = expert_forward(inputs, first_weight[ids_block], first_bias[ids_block], second_weight[ids_block], second_bias[ids_block])[2]
        return (totals + class_sums(logits, labels_block), None)
    totals, _ = lax.scan(first_pass, jnp.zeros((3, NCLS), jnp.float32), (row_inputs, id_grid, row_labels))

    def second_pass(grad_sums, pieces):
        inputs, ids_block, labels_block = pieces
        weights = (first_weight[ids_block], first_bias[ids_block], second_weight[ids_block], second_bias[ids_block])
        grad_inputs, batch_grads = expert_backward(inputs, labels_block, weights, totals, loss_scale)
        owner_hot = (ids_block[:, None] == lax.broadcasted_iota(jnp.int32, (1, EXP), 1)).astype(jnp.float32)
        spread = tuple((jnp.tensordot(owner_hot, piece, axes=((0,), (0,)), precision=lax.Precision.HIGHEST) for piece in batch_grads))
        return (tuple((total + piece for total, piece in zip(grad_sums, spread))), grad_inputs)
    zero_grads = (jnp.zeros((EXP, HIDDEN_SIZE, C), jnp.float32), jnp.zeros((EXP, HIDDEN_SIZE), jnp.float32), jnp.zeros((EXP, NCLS, HIDDEN_SIZE), jnp.float32), jnp.zeros((EXP, NCLS), jnp.float32))
    expert_grads, grad_blocks = lax.scan(second_pass, zero_grads, (row_inputs, id_grid, row_labels))
    grad_act = jnp.transpose(grad_blocks.reshape(NZ, NH, C, W), (2, 0, 1, 3)).astype(jnp.float32)
    grad_pre = (grad_act * silu_grad(conv_pre)).astype(jnp.bfloat16).astype(jnp.float32)
    grad_kernel = jnp.stack([jnp.einsum('ozhw,czhw->oc', grad_pre, shifted(padded, tap_index, NZ, NH, W), precision=lax.Precision.HIGHEST) for tap_index in range(27)])
    denom = totals[1] + totals[2] + 1.0
    dice = (2.0 * totals[0] + 1.0) / denom
    loss = 1.0 - jnp.mean(dice)
    return (loss, grad_kernel, expert_grads[0], expert_grads[1], expert_grads[2], expert_grads[3])
```

```python
import functools
import math

import jax
import jax.numpy as jnp
from jax import lax
from jax.experimental import pallas as pl
from jax.experimental.pallas import tpu as pltpu
from jax.sharding import PartitionSpec as P

MESH = pl.DeviceIdType.MESH
BF16 = jnp.bfloat16
F32 = jnp.float32
I32 = jnp.int32
C = 32
W = 128
HID = 256
NCLS = 117
CLS = 128
ROWS = 16
CAP = 2
BLK = CAP * W
TAPS = 9
GROWS = 16

NT = (((1,), (1,)), ((), ()))
NN = (((1,), (0,)), ((), ()))

HALO = tuple((ds, de) for ds in (-1, 0, 1) for de in (-1, 0, 1) if (ds, de) != (0, 0))


def dot(a, b, dims=NN):
    return lax.dot_general(a, b, dims, preferred_element_type=F32)


def send_part(step, whole):
    return {1: pl.ds(whole, 1), -1: pl.ds(1, 1), 0: pl.ds(1, whole)}[step]


def land_part(step, whole):
    return {1: pl.ds(0, 1), -1: pl.ds(whole + 1, 1), 0: pl.ds(1, whole)}[step]


def body(
    ns, ne,
    x_hbm, k_hbm, lab_hbm, ids_hbm, w1_hbm, b1_hbm, w2_hbm, b2_hbm,
    loss_out, eg_out, gkc_out,
    x_ref, k_ref, lab_ref, ids_ref, w1_ref, b1_ref, w2_ref, b2_ref, in_sem,
    loss_ref, out_sem,
    xf, xp, kwf, kw, x9, act, dconv, lab_ext, lab_snd, lab_rcv, inv,
    w1a, w1t, w2f, w2h, w2t, b2bc, row_snd, row_rcv, xa_all, ha_all, d_all, q_all,
    acc_i, acc_m, acc_c, st1, st2, ab_b, b_b, gl_all, gh_all, ret_snd, ret_rcv, acc_g,
    egf, eg_snd, eg_rcv, eg_all, gp3, gka_snd, gka_rcv, gkb, gkc,
    halo_s, halo_r, lab_s, lab_r, row_s, row_r, st1_s, st1_r, st2_s, st2_r,
    ret_s, ret_r, eg_s, eg_r, ega_s, ega_r, gka_s, gka_r, gkb_s, gkb_r, gkc_s, gkc_r,
):
    me_s = lax.axis_index("slab")
    me_e = lax.axis_index("expert")

    def remote(src, dst, ssem, rsem, s, e):
        return pltpu.make_async_remote_copy(
            src_ref=src, dst_ref=dst, send_sem=ssem, recv_sem=rsem,
            device_id=(s, e), device_id_type=MESH,
        )

    def loop(lo, hi, fn):
        def step(i, carry):
            fn(i)
            return carry
        lax.fori_loop(lo, hi, step, 0)

    def epeer(k):
        return lax.rem(me_e + k, ne)

    def speer(k):
        return lax.rem(me_s + k, ns)

    def exists(ds, de):
        ok = None
        for step, me, n in ((ds, me_s, ns), (de, me_e, ne)):
            if step:
                cond = (me < n - 1) if step > 0 else (me > 0)
                ok = cond if ok is None else jnp.logical_and(ok, cond)
        return ok

    drains = []
    pairs = (
        (x_hbm, x_ref), (ids_hbm, ids_ref), (lab_hbm, lab_ref), (k_hbm, k_ref),
        (w1_hbm, w1_ref), (b1_hbm, b1_ref), (w2_hbm, w2_ref), (b2_hbm, b2_ref),
    )
    loads = [pltpu.make_async_copy(src, dst, in_sem.at[i]) for i, (src, dst) in enumerate(pairs)]
    for load in loads:
        load.start()

    results = ((loss_ref, loss_out), (eg_all, eg_out), (gkc, gkc_out))
    stores = [pltpu.make_async_copy(src, dst, out_sem.at[i]) for i, (src, dst) in enumerate(results)]

    zrow = jnp.zeros((10, C, W), BF16)
    xp[0] = zrow
    xp[3] = zrow
    for z in (1, 2):
        for h in (0, 9):
            xp[z, h] = jnp.zeros((C, W), BF16)

    barrier = pltpu.get_barrier_semaphore()
    loop(1, ne, lambda k: pl.semaphore_signal(barrier, 1, device_id=(me_s, epeer(k)), device_id_type=MESH))
    loop(1, ns, lambda k: pl.semaphore_signal(barrier, 1, device_id=(speer(k), me_e), device_id_type=MESH))
    for ds, de in HALO:
        if ds and de:
            @pl.when(exists(ds, de))
            def _():
                pl.semaphore_signal(barrier, 1, device_id=(me_s + ds, me_e + de), device_id_type=MESH)
    n_s = (me_s > 0).astype(I32) + (me_s < ns - 1).astype(I32)
    n_e = (me_e > 0).astype(I32) + (me_e < ne - 1).astype(I32)

    loads[0].wait()

    xf[...] = x_ref[...].astype(F32)
    for r in range(ROWS):
        xp[1 + r // 8, 1 + r % 8] = xf[pl.ds(r, C, stride=ROWS), :].astype(BF16)

    pl.semaphore_wait(barrier, (ne - 1) + (ns - 1) + n_s * n_e)

    def halo_copy(d, s, e):
        ds, de = HALO[d]
        return remote(
            xp.at[send_part(ds, 2), send_part(de, 8)],
            xp.at[land_part(ds, 2), land_part(de, 8)],
            halo_s.at[d], halo_r.at[d], s, e,
        )

    for d, (ds, de) in enumerate(HALO):
        @pl.when(exists(ds, de))
        def _():
            halo_copy(d, me_s + ds, me_e + de).start()

    loads[1].wait()
    loads[2].wait()

    ids = [ids_ref[r] for r in range(ROWS)]

    def place(e):
        first = jnp.int32(ROWS)
        second = jnp.int32(ROWS)
        for r in reversed(range(ROWS)):
            hit = ids[r] == e
            second = jnp.where(hit, first, second)
            first = jnp.where(hit, jnp.int32(r), first)
        inv[2 * e] = first
        inv[2 * e + 1] = second

    loop(0, ne, place)
    lab_ext[0:ROWS, :] = lab_ref[...]
    lab_ext[ROWS:, :] = jnp.full((8, W), -1, I32)
    act[ROWS] = jnp.zeros((C, W), BF16)

    def put_labels(e):
        lab_snd[e, 0:1] = lab_ext[pl.ds(inv[2 * e], 1), :]
        lab_snd[e, 1:2] = lab_ext[pl.ds(inv[2 * e + 1], 1), :]

    loop(0, ne, put_labels)

    def lab_copy(at, e):
        return remote(lab_snd.at[e], lab_rcv.at[at], lab_s.at[e], lab_r.at[at], me_s, e)

    loop(1, ne, lambda k: lab_copy(me_e, epeer(k)).start())
    lab_rcv[pl.ds(me_e, 1)] = lab_snd[pl.ds(me_e, 1)]

    def drain_halo():
        for d, (ds, de) in enumerate(HALO):
            @pl.when(exists(ds, de))
            def _():
                halo_copy(d, me_s + ds, me_e + de).wait_send()

    drains.append(drain_halo)
    drains.append(lambda: loop(1, ne, lambda k: lab_copy(me_e, epeer(k)).wait_send()))

    for load in loads[3:]:
        load.wait()

    for tap in range(27):
        a, b, c = tap // 9, tap // 3 % 3, tap % 3
        kwf[c * C:(c + 1) * C, (a * 3 + b) * C:(a * 3 + b + 1) * C] = k_ref[tap].astype(F32) * 0.5
    kw[...] = kwf[...].astype(BF16)
    w1 = w1_ref[...].astype(F32) * 0.5
    b1 = b1_ref[...].astype(F32) * 0.5
    w1full = jnp.concatenate([w1, b1, jnp.zeros((CLS - C - 1, HID), F32)], axis=0)
    w1t[...] = w1.astype(BF16)
    w1a[...] = w1full.T.astype(BF16)
    w2f[...] = jnp.zeros((CLS, HID), F32)
    w2f[0:NCLS, :] = w2_ref[...].astype(F32) * 0.5
    w2h[...] = w2f[...].astype(BF16)
    w2t[...] = w2f[...].T.astype(BF16)
    acc_c[0:8, :] = jnp.zeros((8, CLS), F32)
    acc_c[0:1, 0:NCLS] = b2_ref[...].astype(F32) * 0.5
    b2bc[...] = jnp.broadcast_to(acc_c[0:1, :], (CLS, CLS)).T

    classes = lax.broadcasted_iota(I32, (CLS, W), 0)
    lanes = lax.broadcasted_iota(I32, (C, W), 1)
    acc_i[...] = jnp.zeros((CLS, W), F32)
    acc_m[...] = jnp.zeros((CLS, W), F32)
    acc_c[...] = jnp.zeros((CLS, W), F32)
    acc_g[...] = jnp.zeros((CLS, W), F32)

    def count(r):
        acc_c[...] += jnp.where(classes == lab_ext[pl.ds(r, 1), :], 1.0, 0.0)

    loop(0, ROWS, count)

    for d, (ds, de) in enumerate(HALO):
        @pl.when(exists(-ds, -de))
        def _():
            halo_copy(d, me_s - ds, me_e - de).wait_recv()

    def gather(z):
        for h in range(8):
            lane = slice((z * 8 + h) * W, (z * 8 + h + 1) * W)
            for a in range(3):
                x9[a * 96:(a + 1) * 96, lane] = xp[z + a, h:h + 3].reshape(96, W)

    for z in range(2):
        gather(z)

    def conv(p):
        lane = slice(p * BLK, (p + 1) * BLK)
        out = dot(kw[...], x9[:, lane])
        for j in range(2):
            part = out[:, j * W:(j + 1) * W]
            left = jnp.where(lanes > 0, pltpu.roll(part[0:C], 1, 1), 0.0)
            right = jnp.where(lanes < W - 1, pltpu.roll(part[2 * C:3 * C], W - 1, 1), 0.0)
            v = left + part[C:2 * C] + right
            t = jnp.tanh(v)
            act[2 * p + j] = (v + v * t).astype(BF16)
            dconv[2 * p + j] = (1.0 + t) + v * (1.0 - t * t)

    for p in range(ROWS // 2):
        conv(p)

    half = ne // 2

    def turn(i):
        m = (i + 1) // 2
        return half + m * (1 - 2 * lax.rem(i, 2))

    def row_copy(at, e):
        return remote(row_snd.at[e], row_rcv.at[at], row_s.at[e], row_r.at[at], me_s, e)

    def dispatch(i):
        e = epeer(turn(i))
        row_snd[e, 0] = act[inv[2 * e]]
        row_snd[e, 1] = act[inv[2 * e + 1]]
        row_copy(me_e, e).start()

    loop(0, ne - 1, dispatch)
    drains.append(lambda: loop(1, ne, lambda k: row_copy(me_e, epeer(k)).wait_send()))
    row_rcv[me_e, 0] = act[inv[2 * me_e]]
    row_rcv[me_e, 1] = act[inv[2 * me_e + 1]]

    ones = jnp.where(lax.broadcasted_iota(I32, (16, BLK), 0) == 0, 1.0, 0.0).astype(BF16)

    def forward(*blocks):
        ti = acc_i[...]
        tm = acc_m[...]
        for s in blocks:
            col = pl.ds(pl.multiple_of(s * BLK, BLK), BLK)
            x = row_rcv[s]
            xa = jnp.concatenate([jnp.concatenate([x[0], x[1]], axis=1), ones], axis=0)
            xa_all[:, col] = xa
            v = dot(w1a[:, 0:48], xa)
            t = jnp.tanh(v)
            ha = (v + v * t).astype(BF16)
            ha_all[:, col] = ha
            d_all[:, col] = (1.0 + t) + v * (1.0 - t * t)
            z = dot(w2h[...], ha)
            lab = lab_rcv[s]
            for j in range(CAP):
                lj = lab[j:j + 1, :]
                t2 = jnp.tanh(z[:, j * W:(j + 1) * W] + b2bc[...])
                t2 = jnp.where(lj < 0, 1.0, t2)
                q_all[:, pl.ds(pl.multiple_of(s * BLK + j * W, W), W)] = 1.0 - t2 * t2
                ti = ti + jnp.where(classes == lj, t2, 0.0)
                tm = tm + t2
        acc_i[...] = ti
        acc_m[...] = tm

    def arrived(s):
        lab_copy(s, s).wait_recv()
        row_copy(s, s).wait_recv()

    forward(me_e)

    def forward_turn(k):
        before, behind = epeer(ne - k), epeer(k)
        arrived(before)
        arrived(behind)
        forward(before, behind)

    loop(1, half, forward_turn)
    arrived(epeer(half))
    forward(epeer(half))

    def lane_row(m):
        return jnp.sum(m.T, axis=0, keepdims=True)

    st1[pl.ds(me_e, 1)] = jnp.concatenate(
        [lane_row(acc_i[...]), lane_row(acc_m[...]), lane_row(acc_c[...]), jnp.zeros((1, CLS), F32)],
        axis=0,
    )[None]

    def st1_copy(at, e, k):
        return remote(st1.at[at], st1.at[at], st1_s.at[k], st1_r.at[at], me_s, e)

    loop(1, ne, lambda k: st1_copy(me_e, epeer(k), k).start())
    drains.append(lambda: loop(1, ne, lambda k: st1_copy(me_e, epeer(k), k).wait_send()))
    loop(1, ne, lambda k: st1_copy(epeer(k), epeer(k), k).wait_recv())
    st2[pl.ds(me_s, 1)] = jnp.sum(st1[...], axis=0)[None]

    def st2_copy(at, s, k):
        return remote(st2.at[at], st2.at[at], st2_s.at[k], st2_r.at[at], s, me_e)

    loop(1, ns, lambda k: st2_copy(me_s, speer(k), k).start())
    drains.append(lambda: loop(1, ns, lambda k: st2_copy(me_s, speer(k), k).wait_send()))
    loop(1, ns, lambda k: st2_copy(speer(k), speer(k), k).wait_recv())
    sums = jnp.sum(st2[...], axis=0)

    voxels = ns * ne * ROWS * W
    slots = ns * ne * ne * BLK
    scale = 16.0 * NCLS * math.sqrt(voxels)
    cnt = sums[2:3]
    inter = 0.5 * (cnt + sums[0:1])
    mass = 0.5 * sums[1:2] + (voxels - 0.5 * slots)
    denom = mass + cnt + 1.0
    dice = (2.0 * inter + 1.0) / denom
    real = lax.broadcasted_iota(I32, (1, CLS), 1) < NCLS
    loss_ref[...] = 1.0 - jnp.sum(jnp.where(real, dice, 0.0), axis=1, keepdims=True) / NCLS
    coef = jnp.where(real, (0.25 * scale / NCLS) / denom, 0.0)
    ab_b[...] = jnp.broadcast_to(coef * (dice - 2.0), (CLS, CLS)).T
    b_b[...] = jnp.broadcast_to(coef * dice, (CLS, CLS)).T

    def backward(dst, *blocks):
        tg = acc_g[...]
        for s in blocks:
            col = pl.ds(pl.multiple_of(s * BLK, BLK), BLK)
            lab = lab_rcv[s]
            parts = []
            for j in range(CAP):
                eq = classes == lab[j:j + 1, :]
                g = jnp.where(eq, ab_b[...], b_b[...])
                g = g * q_all[:, pl.ds(pl.multiple_of(s * BLK + j * W, W), W)]
                tg = tg + g
                parts.append(g.astype(BF16))
            gl = jnp.concatenate(parts, axis=1)
            gl_all[:, col] = gl
            gh = (dot(w2t[...], gl) * d_all[:, col]).astype(BF16)
            gh_all[:, col] = gh
            gx = dot(w1t[...], gh).astype(BF16)
            dst[s, 0] = gx[:, 0:W]
            dst[s, 1] = gx[:, W:]
        acc_g[...] = tg

    def ret_copy(at, e):
        return remote(ret_snd.at[e], ret_rcv.at[at], ret_s.at[e], ret_r.at[at], me_s, e)

    def backward_turn(i):
        k = half - i
        before, behind = epeer(ne - k), epeer(k)
        backward(ret_snd, before, behind)
        ret_copy(me_e, before).start()
        ret_copy(me_e, behind).start()

    backward(ret_snd, epeer(half))
    ret_copy(me_e, epeer(half)).start()
    loop(1, half, backward_turn)
    drains.append(lambda: loop(1, ne, lambda k: ret_copy(me_e, epeer(k)).wait_send()))
    backward(ret_rcv, me_e)

    egf[:, 0:8, :] = dot(gl_all[...], ha_all[...], NT).reshape(GROWS, 8, HID)
    gw1 = dot(xa_all[...], gh_all[...], NT)
    for i in range(GROWS):
        egf[i, 8:10, :] = gw1[2 * i:2 * i + 2, :]
        egf[i, 10:11, :] = gw1[C:C + 1, :]
        egf[i, 11:16, :] = jnp.zeros((5, HID), F32)
    gb2 = lane_row(acc_g[...])
    egf[0, 11:12, 0:CLS] = gb2
    eg_snd[...] = egf[...].astype(BF16)
    own = GROWS // ns

    def eg_copy(at, s):
        return remote(eg_snd.at[pl.ds(s * own, own)], eg_rcv.at[at], eg_s.at[s], eg_r.at[at], s, me_e)

    loop(1, ns, lambda k: eg_copy(me_s, speer(k)).start())
    drains.append(lambda: loop(1, ns, lambda k: eg_copy(me_s, speer(k)).wait_send()))
    eg_rcv[pl.ds(me_s, 1)] = eg_snd[pl.ds(me_s * own, own)][None]

    loop(1, ne, lambda k: ret_copy(epeer(k), epeer(k)).wait_recv())
    gp3[96:, :] = jnp.zeros((CLS - 96, ROWS * W), BF16)

    def conv_back(r):
        lane = slice(r * W, (r + 1) * W)
        e = ids_ref[r]
        j = jnp.where(inv[2 * e] == r, 0, 1)
        gp = (ret_rcv[e, j].astype(F32) * dconv[r]).astype(BF16).astype(F32)
        gp3[0:C, lane] = jnp.where(lanes < W - 1, pltpu.roll(gp, W - 1, 1), 0.0).astype(BF16)
        gp3[C:2 * C, lane] = gp.astype(BF16)
        gp3[2 * C:3 * C, lane] = jnp.where(lanes > 0, pltpu.roll(gp, 1, 1), 0.0).astype(BF16)

    for r in range(ROWS):
        conv_back(r)
    gkt = dot(x9[...], gp3[...], NT)
    rest = jnp.concatenate([pltpu.roll(gkt[216:], 96 - c * C, 1) for c in range(3)], axis=0)
    full = jnp.where(lax.broadcasted_iota(I32, (216, CLS), 1) < 96, gkt[0:216], rest)
    full = jnp.concatenate([full, jnp.zeros((40, CLS), F32)], axis=0)
    gka_snd[...] = full.astype(BF16).reshape(GROWS, 16, CLS)

    def gka_copy(at, s):
        return remote(gka_snd.at[pl.ds(s * own, own)], gka_rcv.at[at], gka_s.at[s], gka_r.at[at], s, me_e)

    loop(1, ns, lambda k: gka_copy(me_s, speer(k)).start())
    drains.append(lambda: loop(1, ns, lambda k: gka_copy(me_s, speer(k)).wait_send()))
    gka_rcv[pl.ds(me_s, 1)] = gka_snd[pl.ds(me_s * own, own)][None]

    loop(1, ns, lambda k: eg_copy(speer(k), speer(k)).wait_recv())
    eg_all[pl.ds(me_s * own, own)] = jnp.sum(eg_rcv[...].astype(F32), axis=0).astype(BF16)

    def ega_copy(at, s, k):
        part = eg_all.at[pl.ds(at * own, own)]
        return remote(part, part, ega_s.at[k], ega_r.at[at], s, me_e)

    loop(1, ns, lambda k: ega_copy(me_s, speer(k), k).start())
    drains.append(lambda: loop(1, ns, lambda k: ega_copy(me_s, speer(k), k).wait_send()))

    loop(1, ns, lambda k: gka_copy(speer(k), speer(k)).wait_recv())
    gkb[pl.ds(me_e, 1)] = jnp.sum(gka_rcv[...].astype(F32), axis=0).astype(BF16)[None]

    def gkb_copy(at, e, k):
        return remote(gkb.at[at], gkb.at[at], gkb_s.at[k], gkb_r.at[at], me_s, e)

    loop(1, ne, lambda k: gkb_copy(me_e, epeer(k), k).start())
    drains.append(lambda: loop(1, ne, lambda k: gkb_copy(me_e, epeer(k), k).wait_send()))
    loop(1, ne, lambda k: gkb_copy(epeer(k), epeer(k), k).wait_recv())
    gkc[pl.ds(me_s * own, own)] = jnp.sum(gkb[...].astype(F32), axis=0).astype(BF16)

    def gkc_copy(at, s, k):
        part = gkc.at[pl.ds(at * own, own)]
        return remote(part, part, gkc_s.at[k], gkc_r.at[at], s, me_e)

    loop(1, ns, lambda k: gkc_copy(me_s, speer(k), k).start())
    drains.append(lambda: loop(1, ns, lambda k: gkc_copy(me_s, speer(k), k).wait_send()))
    loop(1, ns, lambda k: ega_copy(speer(k), speer(k), k).wait_recv())
    stores[0].start()
    stores[1].start()

    loop(1, ns, lambda k: gkc_copy(speer(k), speer(k), k).wait_recv())
    stores[2].start()
    for drain in drains:
        drain()
    for store in stores:
        store.wait()


def write_out(
    loss_in, eg_in, gkc_in, loss_out, gk_out, gw1_out, gb1_out, gw2_out, gb2_out,
    loss, eg, gkc, gk, gw1, gb1, gw2, gb2, isem, osem,
):
    pairs = ((gkc_in, gkc), (eg_in, eg), (loss_in, loss))
    loads = [pltpu.make_async_copy(src, dst, isem.at[i]) for i, (src, dst) in enumerate(pairs)]
    for load in loads:
        load.start()
    loads[0].wait()
    full = gkc[...].astype(F32).reshape(GROWS * 16, CLS)
    lanes = lax.broadcasted_iota(I32, (72, CLS), 1)
    rest = pltpu.roll(full[0:72], C, 1)
    for c in (1, 2):
        rest = jnp.where(lanes < c * C, rest, pltpu.roll(full[c * 72:(c + 1) * 72], (c + 1) * C, 1))
    gkt = jnp.concatenate([full[0:216], rest], axis=0)
    for j in range(TAPS):
        turned = gkt[j * C:(j + 1) * C]
        turned = jnp.concatenate([turned, jnp.zeros((CLS - C, CLS), F32)], axis=0).T
        for c in range(3):
            gk[3 * j + c] = turned[c * C:(c + 1) * C, 0:C]
    pairs = ((gk, gk_out), (gw1, gw1_out), (gb1, gb1_out), (gw2, gw2_out.at[:, 0, :]), (gb2, gb2_out), (loss, loss_out))
    stores = [pltpu.make_async_copy(src, dst, osem.at[i]) for i, (src, dst) in enumerate(pairs)]
    stores[0].start()
    loads[1].wait()
    loads[2].wait()
    stores[5].start()
    final = eg[...].astype(F32)
    gw2[...] = final[:, 0:8, :].reshape(CLS, HID)[0:NCLS]
    stores[3].start()
    for i in range(GROWS):
        gw1[2 * i:2 * i + 2, :] = final[i, 8:10, :]
    gb1[...] = final[0, 10:11, :]
    gb2[...] = final[0, 11:12, 0:NCLS]
    for i in (1, 2, 4):
        stores[i].start()
    for store in stores:
        store.wait()


def on_device(
    features, kernel, labels, region_ids, first_weight, first_bias, second_weight, second_bias
):
    ns, ne = lax.axis_size("slab"), lax.axis_size("expert")
    cols = ne * BLK
    V = pltpu.VMEM
    own = GROWS // ns
    scratch = [
        V((C * ROWS, W), BF16),
        V((27, C, C), BF16),
        V((ROWS, W), I32),
        pltpu.SMEM((ROWS,), I32),
        V((C, HID), BF16),
        V((1, HID), BF16),
        V((NCLS, HID), BF16),
        V((1, NCLS), BF16),
        pltpu.SemaphoreType.DMA((8,)),
        V((1, 1), F32),
        pltpu.SemaphoreType.DMA((3,)),
        V((C * ROWS, W), F32),
        V((4, 10, C, W), BF16),
        V((3 * C, TAPS * C), F32),
        V((3 * C, TAPS * C), BF16),
        V((TAPS * C, ROWS * W), BF16),
        V((ROWS + 1, C, W), BF16),
        V((ROWS, C, W), F32),
        V((ROWS + 8, W), I32),
        V((ne, CAP, W), I32),
        V((ne, CAP, W), I32),
        pltpu.SMEM((CAP * ne,), I32),
        V((HID, CLS), BF16),
        V((C, HID), BF16),
        V((CLS, HID), F32),
        V((CLS, HID), BF16),
        V((HID, CLS), BF16),
        V((CLS, W), F32),
        V((ne, CAP, C, W), BF16),
        V((ne, CAP, C, W), BF16),
        V((48, cols), BF16),
        V((HID, cols), BF16),
        V((HID, cols), F32),
        V((CLS, cols), F32),
        V((CLS, W), F32),
        V((CLS, W), F32),
        V((CLS, W), F32),
        V((ne, 4, CLS), F32),
        V((ns, 4, CLS), F32),
        V((CLS, W), F32),
        V((CLS, W), F32),
        V((CLS, cols), BF16),
        V((HID, cols), BF16),
        V((ne, CAP, C, W), BF16),
        V((ne, CAP, C, W), BF16),
        V((CLS, W), F32),
        V((GROWS, 16, HID), F32),
        V((GROWS, 16, HID), BF16),
        V((ns, own, 16, HID), BF16),
        V((GROWS, 16, HID), BF16),
        V((CLS, ROWS * W), BF16),
        V((GROWS, 16, CLS), BF16),
        V((ns, own, 16, CLS), BF16),
        V((ne, own, 16, CLS), BF16),
        V((GROWS, 16, CLS), BF16),
    ]
    sems = [8, 8, ne, ne, ne, ne, ne, ne, ns, ns, ne, ne, ns, ns, ns, ns, ns, ns, ne, ne, ns, ns]
    scratch += [pltpu.SemaphoreType.DMA((n,)) for n in sems]
    hbm = pl.BlockSpec(memory_space=pltpu.HBM)
    outs = pl.pallas_call(
        functools.partial(body, ns, ne),
        out_shape=[
            jax.ShapeDtypeStruct((1, 1), F32),
            jax.ShapeDtypeStruct((GROWS, 16, HID), BF16),
            jax.ShapeDtypeStruct((GROWS, 16, CLS), BF16),
        ],
        in_specs=[hbm] * 8,
        out_specs=[hbm] * 3,
        scratch_shapes=scratch,
        compiler_params=pltpu.CompilerParams(
            collective_id=0, has_side_effects=True, vmem_limit_bytes=63 * 2**20
        ),
        name="fused_head",
    )(
        features.reshape(C * ROWS, W),
        kernel,
        labels.reshape(ROWS, W),
        region_ids.reshape(ROWS),
        jnp.swapaxes(first_weight, 1, 2).reshape(C, HID),
        first_bias,
        second_weight.reshape(NCLS, HID),
        second_bias,
    )
    loss, gk, gw1, gb1, gw2, gb2 = pl.pallas_call(
        write_out,
        out_shape=[
            jax.ShapeDtypeStruct((1, 1), F32),
            jax.ShapeDtypeStruct((27, C, C), F32),
            jax.ShapeDtypeStruct((C, HID), F32),
            jax.ShapeDtypeStruct((1, HID), F32),
            jax.ShapeDtypeStruct((NCLS, 1, HID), F32),
            jax.ShapeDtypeStruct((1, NCLS), F32),
        ],
        in_specs=[hbm] * 3,
        out_specs=[hbm] * 6,
        scratch_shapes=[
            V((1, 1), F32),
            V((GROWS, 16, HID), BF16),
            V((GROWS, 16, CLS), BF16),
            V((27, C, C), F32),
            V((C, HID), F32),
            V((1, HID), F32),
            V((NCLS, HID), F32),
            V((1, NCLS), F32),
            pltpu.SemaphoreType.DMA((3,)),
            pltpu.SemaphoreType.DMA((6,)),
        ],
        name="write_out",
    )(*outs)
    return (
        loss.reshape(()),
        gk,
        jnp.swapaxes(gw1.reshape(1, C, HID), 1, 2),
        gb1,
        jnp.swapaxes(gw2, 0, 1),
        gb2,
    )


def solution(mesh):
    in_specs = (
        P(None, "slab", "expert", None),
        P(),
        P("slab", "expert", None),
        P("slab", "expert", None, None),
        P("expert", None, None),
        P("expert", None),
        P("expert", None, None),
        P("expert", None),
    )
    out_specs = (
        P(),
        P(),
        P("expert", None, None),
        P("expert", None),
        P("expert", None, None),
        P("expert", None),
    )
    return jax.shard_map(
        on_device, mesh=mesh, in_specs=in_specs, out_specs=out_specs, check_vma=False
    )
```

```python
import functools
import math

import jax
import jax.numpy as jnp
from jax import lax
from jax.experimental import pallas as pl
from jax.experimental.pallas import tpu as pltpu
from jax.sharding import PartitionSpec as P

MESH = pl.DeviceIdType.MESH
BF16 = jnp.bfloat16
F32 = jnp.float32
I32 = jnp.int32
C = 32
W = 128
HID = 256
NCLS = 117
CLS = 128
ROWS = 16
CAP = 2
BLK = CAP * W
TAPS = 9
GROWS = 16

NT = (((1,), (1,)), ((), ()))
NN = (((1,), (0,)), ((), ()))

HALO = tuple((ds, de) for ds in (-1, 0, 1) for de in (-1, 0, 1) if (ds, de) != (0, 0))


def dot(a, b, dims=NN):
    return lax.dot_general(a, b, dims, preferred_element_type=F32)


def send_part(step, whole):
    return {1: pl.ds(whole, 1), -1: pl.ds(1, 1), 0: pl.ds(1, whole)}[step]


def land_part(step, whole):
    return {1: pl.ds(0, 1), -1: pl.ds(whole + 1, 1), 0: pl.ds(1, whole)}[step]


def body(
    ns, ne,
    x_hbm, k_hbm, lab_hbm, ids_hbm, w1_hbm, b1_hbm, w2_hbm, b2_hbm,
    loss_out, eg_out, gkc_out,
    x_ref, k_ref, lab_ref, ids_ref, w1_ref, b1_ref, w2_ref, b2_ref, in_sem,
    loss_ref, out_sem,
    xf, xp, kwf, kw, x9, act, dconv, lab_ext, lab_snd, lab_rcv, inv,
    w1a, w1t, w2f, w2h, w2t, b2bc, row_snd, row_rcv, xa_all, ha_all, d_all, q_all,
    acc_i, acc_m, acc_c, st1, st2, ab_b, b_b, gl_all, gh_all, ret_snd, ret_rcv, acc_g,
    egf, eg_snd, eg_rcv, eg_all, gp3, gka_snd, gka_rcv, gkb, gkc,
    halo_s, halo_r, lab_s, lab_r, row_s, row_r, st1_s, st1_r, st2_s, st2_r,
    ret_s, ret_r, eg_s, eg_r, ega_s, ega_r, gka_s, gka_r, gkb_s, gkb_r, gkc_s, gkc_r,
):
    me_s = lax.axis_index("slab")
    me_e = lax.axis_index("expert")

    def remote(src, dst, ssem, rsem, s, e):
        return pltpu.make_async_remote_copy(
            src_ref=src, dst_ref=dst, send_sem=ssem, recv_sem=rsem,
            device_id=(s, e), device_id_type=MESH,
        )

    def all_in(ref, sem):
        remote(ref, ref, sem, sem, me_s, epeer(1)).wait_recv()

    def all_out(ref, sem):
        drains.append(lambda: remote(ref, ref, sem, sem, me_s, epeer(1)).wait_send())

    def loop(lo, hi, fn):
        def step(i, carry):
            fn(i)
            return carry
        lax.fori_loop(lo, hi, step, 0)

    def epeer(k):
        return lax.rem(me_e + k, ne)

    def speer(k):
        return lax.rem(me_s + k, ns)

    def exists(ds, de):
        ok = None
        for step, me, n in ((ds, me_s, ns), (de, me_e, ne)):
            if step:
                cond = (me < n - 1) if step > 0 else (me > 0)
                ok = cond if ok is None else jnp.logical_and(ok, cond)
        return ok

    drains = []
    pairs = (
        (x_hbm, x_ref), (ids_hbm, ids_ref), (lab_hbm, lab_ref), (k_hbm, k_ref),
        (w1_hbm, w1_ref), (b1_hbm, b1_ref), (w2_hbm, w2_ref), (b2_hbm, b2_ref),
    )
    loads = [pltpu.make_async_copy(src, dst, in_sem.at[i]) for i, (src, dst) in enumerate(pairs)]
    for load in loads:
        load.start()

    results = ((loss_ref, loss_out), (eg_all, eg_out), (gkc, gkc_out))
    stores = [pltpu.make_async_copy(src, dst, out_sem.at[i]) for i, (src, dst) in enumerate(results)]

    zrow = jnp.zeros((10, C, W), BF16)
    xp[0] = zrow
    xp[3] = zrow
    for z in (1, 2):
        for h in (0, 9):
            xp[z, h] = jnp.zeros((C, W), BF16)

    barrier = pltpu.get_barrier_semaphore()
    loop(1, ne, lambda k: pl.semaphore_signal(barrier, 1, device_id=(me_s, epeer(k)), device_id_type=MESH))
    loop(1, ns, lambda k: pl.semaphore_signal(barrier, 1, device_id=(speer(k), me_e), device_id_type=MESH))
    for ds, de in HALO:
        if ds and de:
            @pl.when(exists(ds, de))
            def _():
                pl.semaphore_signal(barrier, 1, device_id=(me_s + ds, me_e + de), device_id_type=MESH)
    n_s = (me_s > 0).astype(I32) + (me_s < ns - 1).astype(I32)
    n_e = (me_e > 0).astype(I32) + (me_e < ne - 1).astype(I32)

    loads[0].wait()

    xf[...] = x_ref[...].astype(F32)
    for r in range(ROWS):
        xp[1 + r // 8, 1 + r % 8] = xf[pl.ds(r, C, stride=ROWS), :].astype(BF16)

    pl.semaphore_wait(barrier, (ne - 1) + (ns - 1) + n_s * n_e)

    def halo_copy(d, s, e):
        ds, de = HALO[d]
        return remote(
            xp.at[send_part(ds, 2), send_part(de, 8)],
            xp.at[land_part(ds, 2), land_part(de, 8)],
            halo_s.at[d], halo_r.at[d], s, e,
        )

    for d, (ds, de) in enumerate(HALO):
        @pl.when(exists(ds, de))
        def _():
            halo_copy(d, me_s + ds, me_e + de).start()

    loads[1].wait()
    loads[2].wait()

    ids = [ids_ref[r] for r in range(ROWS)]

    def place(e):
        first = jnp.int32(ROWS)
        second = jnp.int32(ROWS)
        for r in reversed(range(ROWS)):
            hit = ids[r] == e
            second = jnp.where(hit, first, second)
            first = jnp.where(hit, jnp.int32(r), first)
        inv[2 * e] = first
        inv[2 * e + 1] = second

    loop(0, ne, place)
    lab_ext[0:ROWS, :] = lab_ref[...]
    lab_ext[ROWS:, :] = jnp.full((8, W), -1, I32)
    act[ROWS] = jnp.zeros((C, W), BF16)

    def put_labels(e):
        lab_snd[e, 0:1] = lab_ext[pl.ds(inv[2 * e], 1), :]
        lab_snd[e, 1:2] = lab_ext[pl.ds(inv[2 * e + 1], 1), :]

    loop(0, ne, put_labels)

    def lab_copy(at, e):
        return remote(lab_snd.at[e], lab_rcv.at[at], lab_s.at[0], lab_r.at[0], me_s, e)

    loop(1, ne, lambda k: lab_copy(me_e, epeer(k)).start())
    lab_rcv[pl.ds(me_e, 1)] = lab_snd[pl.ds(me_e, 1)]

    def drain_halo():
        for d, (ds, de) in enumerate(HALO):
            @pl.when(exists(ds, de))
            def _():
                halo_copy(d, me_s + ds, me_e + de).wait_send()

    drains.append(drain_halo)
    all_out(lab_snd.at[pl.ds(0, ne - 1)], lab_s.at[0])

    for load in loads[3:]:
        load.wait()

    for tap in range(27):
        a, b, c = tap // 9, tap // 3 % 3, tap % 3
        kwf[c * C:(c + 1) * C, (a * 3 + b) * C:(a * 3 + b + 1) * C] = k_ref[tap].astype(F32) * 0.5
    kw[...] = kwf[...].astype(BF16)
    w1 = w1_ref[...].astype(F32) * 0.5
    b1 = b1_ref[...].astype(F32) * 0.5
    w1full = jnp.concatenate([w1, b1, jnp.zeros((CLS - C - 1, HID), F32)], axis=0)
    w1t[...] = w1.astype(BF16)
    w1a[...] = w1full.T.astype(BF16)
    w2f[...] = jnp.zeros((CLS, HID), F32)
    w2f[0:NCLS, :] = w2_ref[...].astype(F32) * 0.5
    w2h[...] = w2f[...].astype(BF16)
    w2t[...] = w2f[...].T.astype(BF16)
    acc_c[0:8, :] = jnp.zeros((8, CLS), F32)
    acc_c[0:1, 0:NCLS] = b2_ref[...].astype(F32) * 0.5
    b2bc[...] = jnp.broadcast_to(acc_c[0:1, :], (CLS, CLS)).T

    classes = lax.broadcasted_iota(I32, (CLS, W), 0)
    lanes = lax.broadcasted_iota(I32, (C, W), 1)
    acc_i[...] = jnp.zeros((CLS, W), F32)
    acc_m[...] = jnp.zeros((CLS, W), F32)
    acc_c[...] = jnp.zeros((CLS, W), F32)
    acc_g[...] = jnp.zeros((CLS, W), F32)

    def count(r):
        acc_c[...] += jnp.where(classes == lab_ext[pl.ds(r, 1), :], 1.0, 0.0)

    loop(0, ROWS, count)

    for d, (ds, de) in enumerate(HALO):
        @pl.when(exists(-ds, -de))
        def _():
            halo_copy(d, me_s - ds, me_e - de).wait_recv()

    def gather(z):
        for h in range(8):
            lane = slice((z * 8 + h) * W, (z * 8 + h + 1) * W)
            for a in range(3):
                x9[a * 96:(a + 1) * 96, lane] = xp[z + a, h:h + 3].reshape(96, W)

    for z in range(2):
        gather(z)

    def conv(p):
        lane = slice(p * BLK, (p + 1) * BLK)
        out = dot(kw[...], x9[:, lane])
        for j in range(2):
            part = out[:, j * W:(j + 1) * W]
            left = jnp.where(lanes > 0, pltpu.roll(part[0:C], 1, 1), 0.0)
            right = jnp.where(lanes < W - 1, pltpu.roll(part[2 * C:3 * C], W - 1, 1), 0.0)
            v = left + part[C:2 * C] + right
            t = jnp.tanh(v)
            act[2 * p + j] = (v + v * t).astype(BF16)
            dconv[2 * p + j] = (1.0 + t) + v * (1.0 - t * t)

    for p in range(ROWS // 2):
        conv(p)

    half = ne // 2

    def turn(i):
        m = i // 2 + 1
        return jnp.where(lax.rem(i, 2) == 0, m, ne - m)

    def row_copy(at, e):
        return remote(row_snd.at[e], row_rcv.at[at], row_s.at[0], row_r.at[at], me_s, e)

    def dispatch(i):
        e = epeer(turn(i))
        row_snd[e, 0] = act[inv[2 * e]]
        row_snd[e, 1] = act[inv[2 * e + 1]]
        row_copy(me_e, e).start()

    loop(0, ne - 1, dispatch)
    all_out(row_snd.at[pl.ds(0, ne - 1)], row_s.at[0])
    row_rcv[me_e, 0] = act[inv[2 * me_e]]
    row_rcv[me_e, 1] = act[inv[2 * me_e + 1]]

    ones = jnp.where(lax.broadcasted_iota(I32, (16, BLK), 0) == 0, 1.0, 0.0).astype(BF16)

    def forward(*blocks):
        ti = acc_i[...]
        tm = acc_m[...]
        for s in blocks:
            col = pl.ds(pl.multiple_of(s * BLK, BLK), BLK)
            x = row_rcv[s]
            xa = jnp.concatenate([jnp.concatenate([x[0], x[1]], axis=1), ones], axis=0)
            xa_all[:, col] = xa
            v = dot(w1a[:, 0:48], xa)
            t = jnp.tanh(v)
            ha = (v + v * t).astype(BF16)
            ha_all[:, col] = ha
            d_all[:, col] = (1.0 + t) + v * (1.0 - t * t)
            z = dot(w2h[...], ha)
            lab = lab_rcv[s]
            for j in range(CAP):
                lj = lab[j:j + 1, :]
                t2 = jnp.tanh(z[:, j * W:(j + 1) * W] + b2bc[...])
                t2 = jnp.where(lj < 0, 1.0, t2)
                q_all[:, pl.ds(pl.multiple_of(s * BLK + j * W, W), W)] = 1.0 - t2 * t2
                ti = ti + jnp.where(classes == lj, t2, 0.0)
                tm = tm + t2
        acc_i[...] = ti
        acc_m[...] = tm

    def arrived(s):
        row_copy(s, s).wait_recv()

    forward(me_e)

    def forward_turn(k):
        before, behind = epeer(ne - k), epeer(k)
        arrived(before)
        arrived(behind)
        forward(before, behind)

    all_in(lab_rcv.at[pl.ds(0, ne - 1)], lab_r.at[0])
    loop(1, half, forward_turn)
    arrived(epeer(half))
    forward(epeer(half))

    def lane_row(m):
        return jnp.sum(m.T, axis=0, keepdims=True)

    st1[pl.ds(me_e, 1)] = jnp.concatenate(
        [lane_row(acc_i[...]), lane_row(acc_m[...]), lane_row(acc_c[...]), jnp.zeros((1, CLS), F32)],
        axis=0,
    )[None]

    def st1_copy(e):
        return remote(st1.at[me_e], st1.at[me_e], st1_s.at[0], st1_r.at[0], me_s, e)

    loop(1, ne, lambda k: st1_copy(epeer(k)).start())
    all_out(st1.at[pl.ds(0, ne - 1)], st1_s.at[0])
    all_in(st1.at[pl.ds(0, ne - 1)], st1_r.at[0])
    st2[pl.ds(me_s, 1)] = jnp.sum(st1[...], axis=0)[None]

    def st2_copy(s):
        return remote(st2.at[me_s], st2.at[me_s], st2_s.at[0], st2_r.at[0], s, me_e)

    loop(1, ns, lambda k: st2_copy(speer(k)).start())
    all_out(st2.at[pl.ds(0, ns - 1)], st2_s.at[0])
    all_in(st2.at[pl.ds(0, ns - 1)], st2_r.at[0])
    sums = jnp.sum(st2[...], axis=0)

    voxels = ns * ne * ROWS * W
    slots = ns * ne * ne * BLK
    scale = 16.0 * NCLS * math.sqrt(voxels)
    cnt = sums[2:3]
    inter = 0.5 * (cnt + sums[0:1])
    mass = 0.5 * sums[1:2] + (voxels - 0.5 * slots)
    denom = mass + cnt + 1.0
    dice = (2.0 * inter + 1.0) / denom
    real = lax.broadcasted_iota(I32, (1, CLS), 1) < NCLS
    loss_ref[...] = 1.0 - jnp.sum(jnp.where(real, dice, 0.0), axis=1, keepdims=True) / NCLS
    coef = jnp.where(real, (0.25 * scale / NCLS) / denom, 0.0)
    ab_b[...] = jnp.broadcast_to(coef * (dice - 2.0), (CLS, CLS)).T
    b_b[...] = jnp.broadcast_to(coef * dice, (CLS, CLS)).T

    def backward(dst, *blocks):
        tg = acc_g[...]
        for s in blocks:
            col = pl.ds(pl.multiple_of(s * BLK, BLK), BLK)
            lab = lab_rcv[s]
            parts = []
            for j in range(CAP):
                eq = classes == lab[j:j + 1, :]
                g = jnp.where(eq, ab_b[...], b_b[...])
                g = g * q_all[:, pl.ds(pl.multiple_of(s * BLK + j * W, W), W)]
                tg = tg + g
                parts.append(g.astype(BF16))
            gl = jnp.concatenate(parts, axis=1)
            gl_all[:, col] = gl
            gh = (dot(w2t[...], gl) * d_all[:, col]).astype(BF16)
            gh_all[:, col] = gh
            gx = dot(w1t[...], gh).astype(BF16)
            dst[s, 0] = gx[:, 0:W]
            dst[s, 1] = gx[:, W:]
        acc_g[...] = tg

    def ret_copy(at, e):
        return remote(ret_snd.at[e], ret_rcv.at[at], ret_s.at[0], ret_r.at[0], me_s, e)

    def backward_turn(i):
        k = half - i
        before, behind = epeer(ne - k), epeer(k)
        backward(ret_snd, before, behind)
        ret_copy(me_e, before).start()
        ret_copy(me_e, behind).start()

    backward(ret_snd, epeer(half))
    ret_copy(me_e, epeer(half)).start()
    loop(1, half, backward_turn)
    all_out(ret_snd.at[pl.ds(0, ne - 1)], ret_s.at[0])
    backward(ret_rcv, me_e)

    egf[:, 0:8, :] = dot(gl_all[...], ha_all[...], NT).reshape(GROWS, 8, HID)
    gw1 = dot(xa_all[...], gh_all[...], NT)
    for i in range(GROWS):
        egf[i, 8:10, :] = gw1[2 * i:2 * i + 2, :]
        egf[i, 10:11, :] = gw1[C:C + 1, :]
        egf[i, 11:16, :] = jnp.zeros((5, HID), F32)
    gb2 = lane_row(acc_g[...])
    egf[0, 11:12, 0:CLS] = gb2
    eg_snd[...] = egf[...].astype(BF16)
    own = GROWS // ns

    def eg_copy(at, s):
        return remote(eg_snd.at[pl.ds(s * own, own)], eg_rcv.at[at], eg_s.at[0], eg_r.at[0], s, me_e)

    loop(1, ns, lambda k: eg_copy(me_s, speer(k)).start())
    all_out(eg_rcv.at[pl.ds(0, ns - 1)], eg_s.at[0])
    eg_rcv[pl.ds(me_s, 1)] = eg_snd[pl.ds(me_s * own, own)][None]

    all_in(ret_rcv.at[pl.ds(0, ne - 1)], ret_r.at[0])
    gp3[96:, :] = jnp.zeros((CLS - 96, ROWS * W), BF16)

    def conv_back(r):
        lane = slice(r * W, (r + 1) * W)
        e = ids_ref[r]
        j = jnp.where(inv[2 * e] == r, 0, 1)
        gp = (ret_rcv[e, j].astype(F32) * dconv[r]).astype(BF16).astype(F32)
        gp3[0:C, lane] = jnp.where(lanes < W - 1, pltpu.roll(gp, W - 1, 1), 0.0).astype(BF16)
        gp3[C:2 * C, lane] = gp.astype(BF16)
        gp3[2 * C:3 * C, lane] = jnp.where(lanes > 0, pltpu.roll(gp, 1, 1), 0.0).astype(BF16)

    for r in range(ROWS):
        conv_back(r)
    gkt = dot(x9[...], gp3[...], NT)
    rest = jnp.concatenate([pltpu.roll(gkt[216:], 96 - c * C, 1) for c in range(3)], axis=0)
    full = jnp.where(lax.broadcasted_iota(I32, (216, CLS), 1) < 96, gkt[0:216], rest)
    full = jnp.concatenate([full, jnp.zeros((40, CLS), F32)], axis=0)
    gka_snd[...] = full.astype(BF16).reshape(GROWS, 16, CLS)

    def gka_copy(at, s):
        return remote(gka_snd.at[pl.ds(s * own, own)], gka_rcv.at[at], gka_s.at[0], gka_r.at[0], s, me_e)

    loop(1, ns, lambda k: gka_copy(me_s, speer(k)).start())
    all_out(gka_rcv.at[pl.ds(0, ns - 1)], gka_s.at[0])
    gka_rcv[pl.ds(me_s, 1)] = gka_snd[pl.ds(me_s * own, own)][None]

    all_in(eg_rcv.at[pl.ds(0, ns - 1)], eg_r.at[0])
    eg_all[pl.ds(me_s * own, own)] = jnp.sum(eg_rcv[...].astype(F32), axis=0).astype(BF16)

    def ega_copy(s):
        part = eg_all.at[pl.ds(me_s * own, own)]
        return remote(part, part, ega_s.at[0], ega_r.at[0], s, me_e)

    loop(1, ns, lambda k: ega_copy(speer(k)).start())
    all_out(eg_all.at[pl.ds(0, (ns - 1) * own)], ega_s.at[0])

    all_in(gka_rcv.at[pl.ds(0, ns - 1)], gka_r.at[0])
    gkb[pl.ds(me_e, 1)] = jnp.sum(gka_rcv[...].astype(F32), axis=0).astype(BF16)[None]

    def gkb_copy(e):
        return remote(gkb.at[me_e], gkb.at[me_e], gkb_s.at[0], gkb_r.at[0], me_s, e)

    loop(1, ne, lambda k: gkb_copy(epeer(k)).start())
    all_out(gkb.at[pl.ds(0, ne - 1)], gkb_s.at[0])
    all_in(gkb.at[pl.ds(0, ne - 1)], gkb_r.at[0])
    gkc[pl.ds(me_s * own, own)] = jnp.sum(gkb[...].astype(F32), axis=0).astype(BF16)

    def gkc_copy(s):
        part = gkc.at[pl.ds(me_s * own, own)]
        return remote(part, part, gkc_s.at[0], gkc_r.at[0], s, me_e)

    loop(1, ns, lambda k: gkc_copy(speer(k)).start())
    all_out(gkc.at[pl.ds(0, (ns - 1) * own)], gkc_s.at[0])
    all_in(eg_all.at[pl.ds(0, (ns - 1) * own)], ega_r.at[0])
    stores[0].start()
    stores[1].start()

    all_in(gkc.at[pl.ds(0, (ns - 1) * own)], gkc_r.at[0])
    stores[2].start()
    for drain in drains:
        drain()
    for store in stores:
        store.wait()


def write_out(
    loss_in, eg_in, gkc_in, loss_out, gk_out, gw1_out, gb1_out, gw2_out, gb2_out,
    loss, eg, gkc, gk, gw1, gb1, gw2, gb2, isem, osem,
):
    pairs = ((gkc_in, gkc), (eg_in, eg), (loss_in, loss))
    loads = [pltpu.make_async_copy(src, dst, isem.at[i]) for i, (src, dst) in enumerate(pairs)]
    for load in loads:
        load.start()
    loads[0].wait()
    full = gkc[...].astype(F32).reshape(GROWS * 16, CLS)
    lanes = lax.broadcasted_iota(I32, (72, CLS), 1)
    rest = pltpu.roll(full[0:72], C, 1)
    for c in (1, 2):
        rest = jnp.where(lanes < c * C, rest, pltpu.roll(full[c * 72:(c + 1) * 72], (c + 1) * C, 1))
    gkt = jnp.concatenate([full[0:216], rest], axis=0)
    for j in range(TAPS):
        turned = gkt[j * C:(j + 1) * C]
        turned = jnp.concatenate([turned, jnp.zeros((CLS - C, CLS), F32)], axis=0).T
        for c in range(3):
            gk[3 * j + c] = turned[c * C:(c + 1) * C, 0:C]
    pairs = ((gk, gk_out), (gw1, gw1_out), (gb1, gb1_out), (gw2, gw2_out.at[:, 0, :]), (gb2, gb2_out), (loss, loss_out))
    stores = [pltpu.make_async_copy(src, dst, osem.at[i]) for i, (src, dst) in enumerate(pairs)]
    stores[0].start()
    loads[1].wait()
    loads[2].wait()
    stores[5].start()
    final = eg[...].astype(F32)
    gw2[...] = final[:, 0:8, :].reshape(CLS, HID)[0:NCLS]
    stores[3].start()
    for i in range(GROWS):
        gw1[2 * i:2 * i + 2, :] = final[i, 8:10, :]
    gb1[...] = final[0, 10:11, :]
    gb2[...] = final[0, 11:12, 0:NCLS]
    for i in (1, 2, 4):
        stores[i].start()
    for store in stores:
        store.wait()


def on_device(
    features, kernel, labels, region_ids, first_weight, first_bias, second_weight, second_bias
):
    ns, ne = lax.axis_size("slab"), lax.axis_size("expert")
    cols = ne * BLK
    V = pltpu.VMEM
    own = GROWS // ns
    scratch = [
        V((C * ROWS, W), BF16),
        V((27, C, C), BF16),
        V((ROWS, W), I32),
        pltpu.SMEM((ROWS,), I32),
        V((C, HID), BF16),
        V((1, HID), BF16),
        V((NCLS, HID), BF16),
        V((1, NCLS), BF16),
        pltpu.SemaphoreType.DMA((8,)),
        V((1, 1), F32),
        pltpu.SemaphoreType.DMA((3,)),
        V((C * ROWS, W), F32),
        V((4, 10, C, W), BF16),
        V((3 * C, TAPS * C), F32),
        V((3 * C, TAPS * C), BF16),
        V((TAPS * C, ROWS * W), BF16),
        V((ROWS + 1, C, W), BF16),
        V((ROWS, C, W), F32),
        V((ROWS + 8, W), I32),
        V((ne, CAP, W), I32),
        V((ne, CAP, W), I32),
        pltpu.SMEM((CAP * ne,), I32),
        V((HID, CLS), BF16),
        V((C, HID), BF16),
        V((CLS, HID), F32),
        V((CLS, HID), BF16),
        V((HID, CLS), BF16),
        V((CLS, W), F32),
        V((ne, CAP, C, W), BF16),
        V((ne, CAP, C, W), BF16),
        V((48, cols), BF16),
        V((HID, cols), BF16),
        V((HID, cols), F32),
        V((CLS, cols), F32),
        V((CLS, W), F32),
        V((CLS, W), F32),
        V((CLS, W), F32),
        V((ne, 4, CLS), F32),
        V((ns, 4, CLS), F32),
        V((CLS, W), F32),
        V((CLS, W), F32),
        V((CLS, cols), BF16),
        V((HID, cols), BF16),
        V((ne, CAP, C, W), BF16),
        V((ne, CAP, C, W), BF16),
        V((CLS, W), F32),
        V((GROWS, 16, HID), F32),
        V((GROWS, 16, HID), BF16),
        V((ns, own, 16, HID), BF16),
        V((GROWS, 16, HID), BF16),
        V((CLS, ROWS * W), BF16),
        V((GROWS, 16, CLS), BF16),
        V((ns, own, 16, CLS), BF16),
        V((ne, own, 16, CLS), BF16),
        V((GROWS, 16, CLS), BF16),
    ]
    sems = [8, 8, 1, 1, 1, ne] + [1] * 16
    scratch += [pltpu.SemaphoreType.DMA((n,)) for n in sems]
    hbm = pl.BlockSpec(memory_space=pltpu.HBM)
    outs = pl.pallas_call(
        functools.partial(body, ns, ne),
        out_shape=[
            jax.ShapeDtypeStruct((1, 1), F32),
            jax.ShapeDtypeStruct((GROWS, 16, HID), BF16),
            jax.ShapeDtypeStruct((GROWS, 16, CLS), BF16),
        ],
        in_specs=[hbm] * 8,
        out_specs=[hbm] * 3,
        scratch_shapes=scratch,
        compiler_params=pltpu.CompilerParams(
            collective_id=0, has_side_effects=True, vmem_limit_bytes=63 * 2**20
        ),
        name="fused_head",
    )(
        features.reshape(C * ROWS, W),
        kernel,
        labels.reshape(ROWS, W),
        region_ids.reshape(ROWS),
        jnp.swapaxes(first_weight, 1, 2).reshape(C, HID),
        first_bias,
        second_weight.reshape(NCLS, HID),
        second_bias,
    )
    loss, gk, gw1, gb1, gw2, gb2 = pl.pallas_call(
        write_out,
        out_shape=[
            jax.ShapeDtypeStruct((1, 1), F32),
            jax.ShapeDtypeStruct((27, C, C), F32),
            jax.ShapeDtypeStruct((C, HID), F32),
            jax.ShapeDtypeStruct((1, HID), F32),
            jax.ShapeDtypeStruct((NCLS, 1, HID), F32),
            jax.ShapeDtypeStruct((1, NCLS), F32),
        ],
        in_specs=[hbm] * 3,
        out_specs=[hbm] * 6,
        scratch_shapes=[
            V((1, 1), F32),
            V((GROWS, 16, HID), BF16),
            V((GROWS, 16, CLS), BF16),
            V((27, C, C), F32),
            V((C, HID), F32),
            V((1, HID), F32),
            V((NCLS, HID), F32),
            V((1, NCLS), F32),
            pltpu.SemaphoreType.DMA((3,)),
            pltpu.SemaphoreType.DMA((6,)),
        ],
        name="write_out",
    )(*outs)
    return (
        loss.reshape(()),
        gk,
        jnp.swapaxes(gw1.reshape(1, C, HID), 1, 2),
        gb1,
        jnp.swapaxes(gw2, 0, 1),
        gb2,
    )


def solution(mesh):
    in_specs = (
        P(None, "slab", "expert", None),
        P(),
        P("slab", "expert", None),
        P("slab", "expert", None, None),
        P("expert", None, None),
        P("expert", None),
        P("expert", None, None),
        P("expert", None),
    )
    out_specs = (
        P(),
        P(),
        P("expert", None, None),
        P("expert", None),
        P("expert", None, None),
        P("expert", None),
    )
    return jax.shard_map(
        on_device, mesh=mesh, in_specs=in_specs, out_specs=out_specs, check_vma=False
    )
```

```python
import functools
import math

import jax
import jax.numpy as jnp
from jax import lax
from jax.experimental import pallas as pl
from jax.experimental.pallas import tpu as pltpu
from jax.sharding import PartitionSpec as P

MESH = pl.DeviceIdType.MESH
BF16 = jnp.bfloat16
F32 = jnp.float32
I32 = jnp.int32
C = 32
W = 128
HID = 256
NCLS = 117
CLS = 128
ROWS = 16
CAP = 2
BLK = CAP * W
TAPS = 9
GROWS = 16

NT = (((1,), (1,)), ((), ()))
NN = (((1,), (0,)), ((), ()))

HALO = ((-1, 0), (1, 0), (-1, -1), (-1, 1), (1, -1), (1, 1), (0, -1), (0, 1))


def dot(a, b, dims=NN):
    return lax.dot_general(a, b, dims, preferred_element_type=F32)


def send_part(step, whole):
    return {1: pl.ds(whole, 1), -1: pl.ds(1, 1), 0: pl.ds(1, whole)}[step]


def land_part(step, whole):
    return {1: pl.ds(0, 1), -1: pl.ds(whole + 1, 1), 0: pl.ds(1, whole)}[step]


def body(
    ns, ne,
    x_hbm, k_hbm, lab_hbm, ids_hbm, w1_hbm, b1_hbm, w2_hbm, b2_hbm,
    loss_out, eg_out, gkc_out,
    x_ref, k_ref, lab_ref, ids_ref, w1_ref, b1_ref, w2_ref, b2_ref, in_sem,
    loss_ref, out_sem,
    xf, xp, kwf, kw, x9, act, dconv, lab_ext, lab_snd, lab_rcv, inv,
    w1a, w1t, w2f, w2h, w2t, b2bc, row_snd, row_rcv, xa_all, ha_all, d_all, q_all,
    acc_i, acc_m, acc_c, st1, st2, ab_b, b_b, gl_all, gh_all, ret_snd, ret_rcv, acc_g,
    egf, eg_snd, eg_rcv, eg_all, gp3, gka_snd, gka_rcv, gkb, gkc,
    halo_s, halo_r, lab_s, lab_r, row_s, row_r, st1_s, st1_r, st2_s, st2_r,
    ret_s, ret_r, eg_s, eg_r, ega_s, ega_r, gka_s, gka_r, gkb_s, gkb_r, gkc_s, gkc_r,
):
    me_s = lax.axis_index("slab")
    me_e = lax.axis_index("expert")

    def remote(src, dst, ssem, rsem, s, e):
        return pltpu.make_async_remote_copy(
            src_ref=src, dst_ref=dst, send_sem=ssem, recv_sem=rsem,
            device_id=(s, e), device_id_type=MESH,
        )

    def all_in(ref, sem):
        remote(ref, ref, sem, sem, me_s, epeer(1)).wait_recv()

    def all_out(ref, sem):
        drains.append(lambda: remote(ref, ref, sem, sem, me_s, epeer(1)).wait_send())

    def loop(lo, hi, fn):
        def step(i, carry):
            fn(i)
            return carry
        lax.fori_loop(lo, hi, step, 0)

    half = ne // 2
    far_e = sorted(range(1, ne), key=lambda k: -min(k, ne - k))
    grid = (4, ns // 4) if ns % 4 == 0 else (1, ns)
    far_s = sorted(
        ((a, b) for a in range(grid[0]) for b in range(grid[1]) if a or b),
        key=lambda p: -min(p[0], grid[0] - p[0]) - min(p[1], grid[1] - p[1]),
    )

    def each_e(fn):
        for k in far_e:
            fn(epeer(k))

    def each_s(fn):
        row, col = me_s // grid[1], lax.rem(me_s, grid[1])
        for a, b in far_s:
            fn(lax.rem(row + a, grid[0]) * grid[1] + lax.rem(col + b, grid[1]))

    def epeer(k):
        return lax.rem(me_e + k, ne)

    def speer(k):
        return lax.rem(me_s + k, ns)

    def exists(ds, de):
        ok = None
        for step, me, n in ((ds, me_s, ns), (de, me_e, ne)):
            if step:
                cond = (me < n - 1) if step > 0 else (me > 0)
                ok = cond if ok is None else jnp.logical_and(ok, cond)
        return ok

    drains = []
    pairs = (
        (x_hbm, x_ref), (ids_hbm, ids_ref), (lab_hbm, lab_ref), (k_hbm, k_ref),
        (w1_hbm, w1_ref), (b1_hbm, b1_ref), (w2_hbm, w2_ref), (b2_hbm, b2_ref),
    )
    loads = [pltpu.make_async_copy(src, dst, in_sem.at[i]) for i, (src, dst) in enumerate(pairs)]
    for load in loads:
        load.start()

    results = ((loss_ref, loss_out), (eg_all, eg_out), (gkc, gkc_out))
    stores = [pltpu.make_async_copy(src, dst, out_sem.at[i]) for i, (src, dst) in enumerate(results)]

    zrow = jnp.zeros((10, C, W), BF16)
    xp[0] = zrow
    xp[3] = zrow
    for z in (1, 2):
        for h in (0, 9):
            xp[z, h] = jnp.zeros((C, W), BF16)

    barrier = pltpu.get_barrier_semaphore()
    each_e(lambda e: pl.semaphore_signal(barrier, 1, device_id=(me_s, e), device_id_type=MESH))
    each_s(lambda s: pl.semaphore_signal(barrier, 1, device_id=(s, me_e), device_id_type=MESH))
    for ds, de in HALO:
        if ds and de:
            @pl.when(exists(ds, de))
            def _():
                pl.semaphore_signal(barrier, 1, device_id=(me_s + ds, me_e + de), device_id_type=MESH)
    n_s = (me_s > 0).astype(I32) + (me_s < ns - 1).astype(I32)
    n_e = (me_e > 0).astype(I32) + (me_e < ne - 1).astype(I32)

    loads[0].wait()

    xf[...] = x_ref[...].astype(F32)
    for r in range(ROWS):
        xp[1 + r // 8, 1 + r % 8] = xf[pl.ds(r, C, stride=ROWS), :].astype(BF16)

    pl.semaphore_wait(barrier, (ne - 1) + (ns - 1) + n_s * n_e)

    def halo_copy(d, s, e):
        ds, de = HALO[d]
        return remote(
            xp.at[send_part(ds, 2), send_part(de, 8)],
            xp.at[land_part(ds, 2), land_part(de, 8)],
            halo_s.at[d], halo_r.at[d], s, e,
        )

    for d, (ds, de) in enumerate(HALO):
        @pl.when(exists(ds, de))
        def _():
            halo_copy(d, me_s + ds, me_e + de).start()

    loads[1].wait()
    loads[2].wait()

    ids = [ids_ref[r] for r in range(ROWS)]

    def place(e):
        first = jnp.int32(ROWS)
        second = jnp.int32(ROWS)
        for r in reversed(range(ROWS)):
            hit = ids[r] == e
            second = jnp.where(hit, first, second)
            first = jnp.where(hit, jnp.int32(r), first)
        inv[2 * e] = first
        inv[2 * e + 1] = second

    loop(0, ne, place)
    lab_ext[0:ROWS, :] = lab_ref[...]
    lab_ext[ROWS:, :] = jnp.full((8, W), -1, I32)
    act[ROWS] = jnp.zeros((C, W), BF16)

    def put_labels(e):
        lab_snd[e, 0:1] = lab_ext[pl.ds(inv[2 * e], 1), :]
        lab_snd[e, 1:2] = lab_ext[pl.ds(inv[2 * e + 1], 1), :]

    loop(0, ne, put_labels)

    def lab_copy(at, e):
        return remote(lab_snd.at[e], lab_rcv.at[at], lab_s.at[0], lab_r.at[0], me_s, e)

    loop(1, ne, lambda k: lab_copy(me_e, epeer(k)).start())
    lab_rcv[pl.ds(me_e, 1)] = lab_snd[pl.ds(me_e, 1)]

    def drain_halo():
        for d, (ds, de) in enumerate(HALO):
            @pl.when(exists(ds, de))
            def _():
                halo_copy(d, me_s + ds, me_e + de).wait_send()

    drains.append(drain_halo)
    all_out(lab_snd.at[pl.ds(0, ne - 1)], lab_s.at[0])

    for load in loads[3:]:
        load.wait()

    for tap in range(27):
        a, b, c = tap // 9, tap // 3 % 3, tap % 3
        kwf[c * C:(c + 1) * C, (a * 3 + b) * C:(a * 3 + b + 1) * C] = k_ref[tap].astype(F32) * 0.5
    kw[...] = kwf[...].astype(BF16)
    w1 = w1_ref[...].astype(F32) * 0.5
    b1 = b1_ref[...].astype(F32) * 0.5
    w1full = jnp.concatenate([w1, b1, jnp.zeros((CLS - C - 1, HID), F32)], axis=0)
    w1t[...] = w1.astype(BF16)
    w1a[...] = w1full.T.astype(BF16)
    w2f[...] = jnp.zeros((CLS, HID), F32)
    w2f[0:NCLS, :] = w2_ref[...].astype(F32) * 0.5
    w2h[...] = w2f[...].astype(BF16)
    w2t[...] = w2f[...].T.astype(BF16)
    acc_c[0:8, :] = jnp.zeros((8, CLS), F32)
    acc_c[0:1, 0:NCLS] = b2_ref[...].astype(F32) * 0.5
    b2bc[...] = jnp.broadcast_to(acc_c[0:1, :], (CLS, CLS)).T

    classes = lax.broadcasted_iota(I32, (CLS, W), 0)
    lanes = lax.broadcasted_iota(I32, (C, W), 1)
    acc_i[...] = jnp.zeros((CLS, W), F32)
    acc_m[...] = jnp.zeros((CLS, W), F32)
    acc_c[...] = jnp.zeros((CLS, W), F32)
    acc_g[...] = jnp.zeros((CLS, W), F32)

    def count(r):
        acc_c[...] += jnp.where(classes == lab_ext[pl.ds(r, 1), :], 1.0, 0.0)

    loop(0, ROWS, count)
    x9[TAPS * C:, :] = jnp.zeros((96, ROWS * W), BF16)

    for d, (ds, de) in enumerate(HALO):
        @pl.when(exists(-ds, -de))
        def _():
            halo_copy(d, me_s - ds, me_e - de).wait_recv()

    def gather(z):
        for h in range(8):
            lane = slice((z * 8 + h) * W, (z * 8 + h + 1) * W)
            for a in range(3):
                x9[a * 96:(a + 1) * 96, lane] = xp[z + a, h:h + 3].reshape(96, W)

    for z in range(2):
        gather(z)

    def conv(p):
        lane = slice(p * BLK, (p + 1) * BLK)
        out = dot(kw[...], x9[0:TAPS * C, lane])
        for j in range(2):
            part = out[:, j * W:(j + 1) * W]
            left = jnp.where(lanes > 0, pltpu.roll(part[0:C], 1, 1), 0.0)
            right = jnp.where(lanes < W - 1, pltpu.roll(part[2 * C:3 * C], W - 1, 1), 0.0)
            v = left + part[C:2 * C] + right
            t = jnp.tanh(v)
            act[2 * p + j] = (v + v * t).astype(BF16)
            dconv[2 * p + j] = (1.0 + t) + v * (1.0 - t * t)

    for p in range(ROWS // 2):
        conv(p)

    def turn(i):
        m = i // 2 + 1
        return jnp.where(lax.rem(i, 2) == 0, m, ne - m)

    def row_copy(at, e):
        return remote(row_snd.at[e], row_rcv.at[at], row_s.at[0], row_r.at[at], me_s, e)

    def dispatch(i):
        e = epeer(turn(i))
        row_snd[e, 0] = act[inv[2 * e]]
        row_snd[e, 1] = act[inv[2 * e + 1]]
        row_copy(me_e, e).start()

    loop(0, ne - 1, dispatch)
    all_out(row_snd.at[pl.ds(0, ne - 1)], row_s.at[0])
    row_rcv[me_e, 0] = act[inv[2 * me_e]]
    row_rcv[me_e, 1] = act[inv[2 * me_e + 1]]

    ones = jnp.where(lax.broadcasted_iota(I32, (16, BLK), 0) == 0, 1.0, 0.0).astype(BF16)

    def forward(*blocks):
        ti = acc_i[...]
        tm = acc_m[...]
        for s in blocks:
            col = pl.ds(pl.multiple_of(s * BLK, BLK), BLK)
            x = row_rcv[s]
            xa = jnp.concatenate([jnp.concatenate([x[0], x[1]], axis=1), ones], axis=0)
            xa_all[:, col] = xa
            v = dot(w1a[:, 0:48], xa)
            t = jnp.tanh(v)
            ha = (v + v * t).astype(BF16)
            ha_all[:, col] = ha
            d_all[:, col] = (1.0 + t) + v * (1.0 - t * t)
            z = dot(w2h[...], ha)
            lab = lab_rcv[s]
            for j in range(CAP):
                lj = lab[j:j + 1, :]
                t2 = jnp.tanh(z[:, j * W:(j + 1) * W] + b2bc[...])
                t2 = jnp.where(lj < 0, 1.0, t2)
                q_all[:, pl.ds(pl.multiple_of(s * BLK + j * W, W), W)] = 1.0 - t2 * t2
                ti = ti + jnp.where(classes == lj, t2, 0.0)
                tm = tm + t2
        acc_i[...] = ti
        acc_m[...] = tm

    def arrived(s):
        row_copy(s, s).wait_recv()

    forward(me_e)

    def forward_turn(k):
        before, behind = epeer(ne - k), epeer(k)
        arrived(before)
        arrived(behind)
        forward(before, behind)

    all_in(lab_rcv.at[pl.ds(0, ne - 1)], lab_r.at[0])
    loop(1, half, forward_turn)
    arrived(epeer(half))
    forward(epeer(half))

    def lane_row(m):
        return jnp.sum(m.T, axis=0, keepdims=True)

    st1[pl.ds(me_e, 1)] = jnp.concatenate(
        [lane_row(acc_i[...]), lane_row(acc_m[...]), lane_row(acc_c[...]), jnp.zeros((1, CLS), F32)],
        axis=0,
    )[None]

    def st1_copy(e):
        return remote(st1.at[me_e], st1.at[me_e], st1_s.at[0], st1_r.at[0], me_s, e)

    each_e(lambda e: st1_copy(e).start())
    all_out(st1.at[pl.ds(0, ne - 1)], st1_s.at[0])
    all_in(st1.at[pl.ds(0, ne - 1)], st1_r.at[0])
    st2[pl.ds(me_s, 1)] = jnp.sum(st1[...], axis=0)[None]

    def st2_copy(s):
        return remote(st2.at[me_s], st2.at[me_s], st2_s.at[0], st2_r.at[0], s, me_e)

    each_s(lambda s: st2_copy(s).start())
    all_out(st2.at[pl.ds(0, ns - 1)], st2_s.at[0])
    all_in(st2.at[pl.ds(0, ns - 1)], st2_r.at[0])
    sums = jnp.sum(st2[...], axis=0)

    voxels = ns * ne * ROWS * W
    slots = ns * ne * ne * BLK
    scale = 16.0 * NCLS * math.sqrt(voxels)
    cnt = sums[2:3]
    inter = 0.5 * (cnt + sums[0:1])
    mass = 0.5 * sums[1:2] + (voxels - 0.5 * slots)
    denom = mass + cnt + 1.0
    dice = (2.0 * inter + 1.0) / denom
    real = lax.broadcasted_iota(I32, (1, CLS), 1) < NCLS
    loss_ref[...] = 1.0 - jnp.sum(jnp.where(real, dice, 0.0), axis=1, keepdims=True) / NCLS
    coef = jnp.where(real, (0.25 * scale / NCLS) / denom, 0.0)
    ab_b[...] = jnp.broadcast_to(coef * (dice - 2.0), (CLS, CLS)).T
    b_b[...] = jnp.broadcast_to(coef * dice, (CLS, CLS)).T

    def backward(dst, *blocks):
        tg = acc_g[...]
        for s in blocks:
            col = pl.ds(pl.multiple_of(s * BLK, BLK), BLK)
            lab = lab_rcv[s]
            parts = []
            for j in range(CAP):
                eq = classes == lab[j:j + 1, :]
                g = jnp.where(eq, ab_b[...], b_b[...])
                g = g * q_all[:, pl.ds(pl.multiple_of(s * BLK + j * W, W), W)]
                tg = tg + g
                parts.append(g.astype(BF16))
            gl = jnp.concatenate(parts, axis=1)
            gl_all[:, col] = gl
            for c in range(0, HID, 64):
                gh_all[c:c + 64, col] = (dot(w2t[c:c + 64, :], gl) * d_all[c:c + 64, col]).astype(BF16)
            gx = dot(w1t[...], gh_all[:, col]).astype(BF16)
            dst[s, 0] = gx[:, 0:W]
            dst[s, 1] = gx[:, W:]
        acc_g[...] = tg

    def ret_copy(at, e):
        return remote(ret_snd.at[e], ret_rcv.at[at], ret_s.at[0], ret_r.at[0], me_s, e)

    def backward_turn(i):
        k = half - i
        before, behind = epeer(ne - k), epeer(k)
        backward(ret_snd, before, behind)
        ret_copy(me_e, before).start()
        ret_copy(me_e, behind).start()

    backward(ret_snd, epeer(half))
    ret_copy(me_e, epeer(half)).start()
    loop(1, half, backward_turn)
    all_out(ret_snd.at[pl.ds(0, ne - 1)], ret_s.at[0])
    backward(ret_rcv, me_e)

    egf[:, 0:8, :] = dot(gl_all[...], ha_all[...], NT).reshape(GROWS, 8, HID)
    gw1 = dot(xa_all[...], gh_all[...], NT)
    for i in range(GROWS):
        egf[i, 8:10, :] = gw1[2 * i:2 * i + 2, :]
        egf[i, 10:11, :] = gw1[C:C + 1, :]
        egf[i, 11:16, :] = jnp.zeros((5, HID), F32)
    gb2 = lane_row(acc_g[...])
    egf[0, 11:12, 0:CLS] = gb2
    eg_snd[...] = egf[...].astype(BF16)
    own = GROWS // ns

    def eg_copy(at, s):
        return remote(eg_snd.at[pl.ds(s * own, own)], eg_rcv.at[at], eg_s.at[0], eg_r.at[0], s, me_e)

    loop(1, ns, lambda k: eg_copy(me_s, speer(k)).start())
    all_out(eg_rcv.at[pl.ds(0, ns - 1)], eg_s.at[0])
    eg_rcv[pl.ds(me_s, 1)] = eg_snd[pl.ds(me_s * own, own)][None]

    all_in(ret_rcv.at[pl.ds(0, ne - 1)], ret_r.at[0])

    def conv_back(r):
        lane = slice(r * W, (r + 1) * W)
        e = ids_ref[r]
        j = jnp.where(inv[2 * e] == r, 0, 1)
        gp = (ret_rcv[e, j].astype(F32) * dconv[r]).astype(BF16).astype(F32)
        gp3[0:C, lane] = jnp.where(lanes < W - 1, pltpu.roll(gp, W - 1, 1), 0.0).astype(BF16)
        gp3[C:2 * C, lane] = gp.astype(BF16)
        gp3[2 * C:3 * C, lane] = jnp.where(lanes > 0, pltpu.roll(gp, 1, 1), 0.0).astype(BF16)

    for r in range(ROWS):
        conv_back(r)
    gkt = dot(gp3[...], x9[...], NT)
    tail = gkt[:, 256:]
    rest = tail[0:24]
    for g in range(1, 4):
        rest = rest + pltpu.roll(tail[24 * g:24 * g + 24], C * g, 1)
    full = jnp.concatenate([gkt[:, 0:128], gkt[:, 128:256], rest, jnp.zeros((40, CLS), F32)], axis=0)
    gka_snd[...] = full.astype(BF16).reshape(GROWS, 16, CLS)

    def gka_copy(at, s):
        return remote(gka_snd.at[pl.ds(s * own, own)], gka_rcv.at[at], gka_s.at[0], gka_r.at[0], s, me_e)

    each_s(lambda s: gka_copy(me_s, s).start())
    all_out(gka_rcv.at[pl.ds(0, ns - 1)], gka_s.at[0])
    gka_rcv[pl.ds(me_s, 1)] = gka_snd[pl.ds(me_s * own, own)][None]

    all_in(gka_rcv.at[pl.ds(0, ns - 1)], gka_r.at[0])
    gkb[pl.ds(me_e, 1)] = jnp.sum(gka_rcv[...].astype(F32), axis=0).astype(BF16)[None]

    def gkb_copy(e):
        return remote(gkb.at[me_e], gkb.at[me_e], gkb_s.at[0], gkb_r.at[0], me_s, e)

    each_e(lambda e: gkb_copy(e).start())
    all_out(gkb.at[pl.ds(0, ne - 1)], gkb_s.at[0])

    all_in(eg_rcv.at[pl.ds(0, ns - 1)], eg_r.at[0])
    eg_all[pl.ds(me_s * own, own)] = jnp.sum(eg_rcv[...].astype(F32), axis=0).astype(BF16)

    def ega_copy(s):
        part = eg_all.at[pl.ds(me_s * own, own)]
        return remote(part, part, ega_s.at[0], ega_r.at[0], s, me_e)

    loop(1, ns, lambda k: ega_copy(speer(k)).start())
    all_out(eg_all.at[pl.ds(0, (ns - 1) * own)], ega_s.at[0])

    all_in(gkb.at[pl.ds(0, ne - 1)], gkb_r.at[0])
    gkc[pl.ds(me_s * own, own)] = jnp.sum(gkb[...].astype(F32), axis=0).astype(BF16)

    def gkc_copy(s):
        part = gkc.at[pl.ds(me_s * own, own)]
        return remote(part, part, gkc_s.at[0], gkc_r.at[0], s, me_e)

    each_s(lambda s: gkc_copy(s).start())
    all_out(gkc.at[pl.ds(0, (ns - 1) * own)], gkc_s.at[0])
    all_in(eg_all.at[pl.ds(0, (ns - 1) * own)], ega_r.at[0])
    stores[0].start()
    stores[1].start()

    all_in(gkc.at[pl.ds(0, (ns - 1) * own)], gkc_r.at[0])
    stores[2].start()
    for drain in drains:
        drain()
    for store in stores:
        store.wait()


def write_out(
    loss_in, eg_in, gkc_in, loss_out, gk_out, gw1_out, gb1_out, gw2_out, gb2_out,
    loss, eg, gkc, gk, gw1, gb1, gw2, gb2, isem, osem,
):
    pairs = ((gkc_in, gkc), (eg_in, eg), (loss_in, loss))
    loads = [pltpu.make_async_copy(src, dst, isem.at[i]) for i, (src, dst) in enumerate(pairs)]
    for load in loads:
        load.start()
    loads[0].wait()
    full = gkc[...].astype(F32).reshape(GROWS * 16, CLS)
    rest = jnp.concatenate([full[192:216]] + [pltpu.roll(full[192:216], CLS - C * g, 1) for g in range(1, 4)], axis=0)
    for j in range(TAPS):
        turned = full[j // 4 * 96:j // 4 * 96 + 96] if j < 8 else rest
        if j % 4:
            turned = pltpu.roll(turned, CLS - C * (j % 4), 1)
        for c in range(3):
            gk[3 * j + c] = turned[c * C:(c + 1) * C, 0:C]
    pairs = ((gk, gk_out), (gw1, gw1_out), (gb1, gb1_out), (gw2, gw2_out.at[:, 0, :]), (gb2, gb2_out), (loss, loss_out))
    stores = [pltpu.make_async_copy(src, dst, osem.at[i]) for i, (src, dst) in enumerate(pairs)]
    stores[0].start()
    loads[1].wait()
    loads[2].wait()
    stores[5].start()
    final = eg[...].astype(F32)
    gw2[...] = final[:, 0:8, :].reshape(CLS, HID)[0:NCLS]
    stores[3].start()
    for i in range(GROWS):
        gw1[2 * i:2 * i + 2, :] = final[i, 8:10, :]
    gb1[...] = final[0, 10:11, :]
    gb2[...] = final[0, 11:12, 0:NCLS]
    for i in (1, 2, 4):
        stores[i].start()
    for store in stores:
        store.wait()


def on_device(
    features, kernel, labels, region_ids, first_weight, first_bias, second_weight, second_bias
):
    ns, ne = lax.axis_size("slab"), lax.axis_size("expert")
    cols = ne * BLK
    V = pltpu.VMEM
    own = GROWS // ns
    scratch = [
        V((C * ROWS, W), BF16),
        V((27, C, C), BF16),
        V((ROWS, W), I32),
        pltpu.SMEM((ROWS,), I32),
        V((C, HID), BF16),
        V((1, HID), BF16),
        V((NCLS, HID), BF16),
        V((1, NCLS), BF16),
        pltpu.SemaphoreType.DMA((8,)),
        V((1, 1), F32),
        pltpu.SemaphoreType.DMA((3,)),
        V((C * ROWS, W), F32),
        V((4, 10, C, W), BF16),
        V((3 * C, TAPS * C), F32),
        V((3 * C, TAPS * C), BF16),
        V((384, ROWS * W), BF16),
        V((ROWS + 1, C, W), BF16),
        V((ROWS, C, W), F32),
        V((ROWS + 8, W), I32),
        V((ne, CAP, W), I32),
        V((ne, CAP, W), I32),
        pltpu.SMEM((CAP * ne,), I32),
        V((HID, CLS), BF16),
        V((C, HID), BF16),
        V((CLS, HID), F32),
        V((CLS, HID), BF16),
        V((HID, CLS), BF16),
        V((CLS, W), F32),
        V((ne, CAP, C, W), BF16),
        V((ne, CAP, C, W), BF16),
        V((48, cols), BF16),
        V((HID, cols), BF16),
        V((HID, cols), F32),
        V((CLS, cols), F32),
        V((CLS, W), F32),
        V((CLS, W), F32),
        V((CLS, W), F32),
        V((ne, 4, CLS), F32),
        V((ns, 4, CLS), F32),
        V((CLS, W), F32),
        V((CLS, W), F32),
        V((CLS, cols), BF16),
        V((HID, cols), BF16),
        V((ne, CAP, C, W), BF16),
        V((ne, CAP, C, W), BF16),
        V((CLS, W), F32),
        V((GROWS, 16, HID), F32),
        V((GROWS, 16, HID), BF16),
        V((ns, own, 16, HID), BF16),
        V((GROWS, 16, HID), BF16),
        V((96, ROWS * W), BF16),
        V((GROWS, 16, CLS), BF16),
        V((ns, own, 16, CLS), BF16),
        V((ne, own, 16, CLS), BF16),
        V((GROWS, 16, CLS), BF16),
    ]
    sems = [8, 8, 1, 1, 1, ne] + [1] * 16
    scratch += [pltpu.SemaphoreType.DMA((n,)) for n in sems]
    hbm = pl.BlockSpec(memory_space=pltpu.HBM)
    outs = pl.pallas_call(
        functools.partial(body, ns, ne),
        out_shape=[
            jax.ShapeDtypeStruct((1, 1), F32),
            jax.ShapeDtypeStruct((GROWS, 16, HID), BF16),
            jax.ShapeDtypeStruct((GROWS, 16, CLS), BF16),
        ],
        in_specs=[hbm] * 8,
        out_specs=[hbm] * 3,
        scratch_shapes=scratch,
        compiler_params=pltpu.CompilerParams(
            collective_id=0, has_side_effects=True, vmem_limit_bytes=63 * 2**20
        ),
        name="fused_head",
    )(
        features.reshape(C * ROWS, W),
        kernel,
        labels.reshape(ROWS, W),
        region_ids.reshape(ROWS),
        jnp.swapaxes(first_weight, 1, 2).reshape(C, HID),
        first_bias,
        second_weight.reshape(NCLS, HID),
        second_bias,
    )
    loss, gk, gw1, gb1, gw2, gb2 = pl.pallas_call(
        write_out,
        out_shape=[
            jax.ShapeDtypeStruct((1, 1), F32),
            jax.ShapeDtypeStruct((27, C, C), F32),
            jax.ShapeDtypeStruct((C, HID), F32),
            jax.ShapeDtypeStruct((1, HID), F32),
            jax.ShapeDtypeStruct((NCLS, 1, HID), F32),
            jax.ShapeDtypeStruct((1, NCLS), F32),
        ],
        in_specs=[hbm] * 3,
        out_specs=[hbm] * 6,
        scratch_shapes=[
            V((1, 1), F32),
            V((GROWS, 16, HID), BF16),
            V((GROWS, 16, CLS), BF16),
            V((27, C, C), F32),
            V((C, HID), F32),
            V((1, HID), F32),
            V((NCLS, HID), F32),
            V((1, NCLS), F32),
            pltpu.SemaphoreType.DMA((3,)),
            pltpu.SemaphoreType.DMA((6,)),
        ],
        name="write_out",
    )(*outs)
    return (
        loss.reshape(()),
        gk,
        jnp.swapaxes(gw1.reshape(1, C, HID), 1, 2),
        gb1,
        jnp.swapaxes(gw2, 0, 1),
        gb2,
    )


def solution(mesh):
    in_specs = (
        P(None, "slab", "expert", None),
        P(),
        P("slab", "expert", None),
        P("slab", "expert", None, None),
        P("expert", None, None),
        P("expert", None),
        P("expert", None, None),
        P("expert", None),
    )
    out_specs = (
        P(),
        P(),
        P("expert", None, None),
        P("expert", None),
        P("expert", None, None),
        P("expert", None),
    )
    return jax.shard_map(
        on_device, mesh=mesh, in_specs=in_specs, out_specs=out_specs, check_vma=False
    )
```

```python
import functools
import math

import jax
import jax.numpy as jnp
from jax import lax
from jax.experimental import pallas as pl
from jax.experimental.pallas import tpu as pltpu
from jax.sharding import PartitionSpec as P

MESH = pl.DeviceIdType.MESH
BF16 = jnp.bfloat16
F32 = jnp.float32
I32 = jnp.int32
C = 32
W = 128
HID = 256
NCLS = 117
CLS = 128
ROWS = 16
CAP = 2
BLK = CAP * W
TAPS = 9
GROWS = 16

NT = (((1,), (1,)), ((), ()))
NN = (((1,), (0,)), ((), ()))

HALO = ((-1, 0), (1, 0), (-1, -1), (-1, 1), (1, -1), (1, 1), (0, -1), (0, 1))


def dot(a, b, dims=NN):
    return lax.dot_general(a, b, dims, preferred_element_type=F32)


def send_part(step, whole):
    return {1: pl.ds(whole, 1), -1: pl.ds(1, 1), 0: pl.ds(1, whole)}[step]


def land_part(step, whole):
    return {1: pl.ds(0, 1), -1: pl.ds(whole + 1, 1), 0: pl.ds(1, whole)}[step]


def body(
    ns, ne,
    x_hbm, k_hbm, lab_hbm, ids_hbm, w1_hbm, b1_hbm, w2_hbm, b2_hbm,
    loss_out, eg_out, gkc_out,
    x_ref, k_ref, lab_ref, ids_ref, w1_ref, b1_ref, w2_ref, b2_ref, in_sem,
    loss_ref, out_sem,
    xf, xp, kwf, kw, x9, act, dconv, lab_ext, lab_snd, lab_rcv, inv,
    w1a, w1t, w2f, w2h, w2t, b2bc, row_snd, row_rcv, xa_all, ha_all, d_all, q_all,
    acc_i, acc_m, acc_c, st1, st2, ab_b, b_b, gl_all, gh_all, ret_snd, ret_rcv, acc_g,
    egf, eg_snd, eg_rcv, eg_all, gp3, gka_snd, gka_rcv, gkb, gkc,
    halo_s, halo_r, lab_s, lab_r, row_s, row_r, st1_s, st1_r, st2_s, st2_r,
    ret_s, ret_r, eg_s, eg_r, ega_s, ega_r, gka_s, gka_r, gkb_s, gkb_r, gkc_s, gkc_r,
):
    me_s = lax.axis_index("slab")
    me_e = lax.axis_index("expert")

    def remote(src, dst, ssem, rsem, s, e):
        return pltpu.make_async_remote_copy(
            src_ref=src, dst_ref=dst, send_sem=ssem, recv_sem=rsem,
            device_id=(s, e), device_id_type=MESH,
        )

    def all_in(ref, sem):
        remote(ref, ref, sem, sem, me_s, epeer(1)).wait_recv()

    def all_out(ref, sem):
        drains.append(lambda: remote(ref, ref, sem, sem, me_s, epeer(1)).wait_send())

    def loop(lo, hi, fn):
        def step(i, carry):
            fn(i)
            return carry
        lax.fori_loop(lo, hi, step, 0)

    half = ne // 2
    far_e = sorted(range(1, ne), key=lambda k: -min(k, ne - k))
    grid = (4, ns // 4) if ns % 4 == 0 else (1, ns)
    far_s = sorted(
        ((a, b) for a in range(grid[0]) for b in range(grid[1]) if a or b),
        key=lambda p: -min(p[0], grid[0] - p[0]) - min(p[1], grid[1] - p[1]),
    )

    def each_e(fn):
        for k in far_e:
            fn(epeer(k))

    def each_s(fn):
        row, col = me_s // grid[1], lax.rem(me_s, grid[1])
        for a, b in far_s:
            fn(lax.rem(row + a, grid[0]) * grid[1] + lax.rem(col + b, grid[1]))

    def epeer(k):
        return lax.rem(me_e + k, ne)

    def speer(k):
        return lax.rem(me_s + k, ns)

    def exists(ds, de):
        ok = None
        for step, me, n in ((ds, me_s, ns), (de, me_e, ne)):
            if step:
                cond = (me < n - 1) if step > 0 else (me > 0)
                ok = cond if ok is None else jnp.logical_and(ok, cond)
        return ok

    drains = []
    pairs = (
        (x_hbm, x_ref), (ids_hbm, ids_ref), (lab_hbm, lab_ref), (k_hbm, k_ref),
        (w1_hbm, w1_ref), (b1_hbm, b1_ref), (w2_hbm, w2_ref), (b2_hbm, b2_ref),
    )
    loads = [pltpu.make_async_copy(src, dst, in_sem.at[i]) for i, (src, dst) in enumerate(pairs)]
    loads[0].start()

    results = ((loss_ref, loss_out), (eg_all, eg_out), (gkc, gkc_out))
    stores = [pltpu.make_async_copy(src, dst, out_sem.at[i]) for i, (src, dst) in enumerate(results)]

    zrow = jnp.zeros((10, C, W), BF16)
    xp[0] = zrow
    xp[3] = zrow
    for z in (1, 2):
        for h in (0, 9):
            xp[z, h] = jnp.zeros((C, W), BF16)

    barrier = pltpu.get_barrier_semaphore()
    def hello(s, e):
        pl.semaphore_signal(barrier, 1, device_id=(s, e), device_id_type=MESH)

    hellos = []
    each_e(lambda e: hellos.append((me_s, e)))
    each_s(lambda s: hellos.append((s, me_e)))
    for i in range(ne - 1 + ns - 1):
        at = i // 2 if i % 2 == 0 else ne - 1 + i // 2
        hello(*hellos[at if ns == ne else i])
    for ds, de in HALO:
        if ds and de:
            @pl.when(exists(ds, de))
            def _():
                hello(me_s + ds, me_e + de)
    for load in loads[1:]:
        load.start()
    n_s = (me_s > 0).astype(I32) + (me_s < ns - 1).astype(I32)
    n_e = (me_e > 0).astype(I32) + (me_e < ne - 1).astype(I32)

    loads[0].wait()

    xf[...] = x_ref[...].astype(F32)
    for r in range(ROWS):
        xp[1 + r // 8, 1 + r % 8] = xf[pl.ds(r, C, stride=ROWS), :].astype(BF16)

    pl.semaphore_wait(barrier, (ne - 1) + (ns - 1) + n_s * n_e)

    def halo_copy(d, s, e):
        ds, de = HALO[d]
        return remote(
            xp.at[send_part(ds, 2), send_part(de, 8)],
            xp.at[land_part(ds, 2), land_part(de, 8)],
            halo_s.at[d], halo_r.at[d], s, e,
        )

    for d, (ds, de) in enumerate(HALO):
        @pl.when(exists(ds, de))
        def _():
            halo_copy(d, me_s + ds, me_e + de).start()

    loads[1].wait()
    loads[2].wait()

    ids = [ids_ref[r] for r in range(ROWS)]

    def place(e):
        first = jnp.int32(ROWS)
        second = jnp.int32(ROWS)
        for r in reversed(range(ROWS)):
            hit = ids[r] == e
            second = jnp.where(hit, first, second)
            first = jnp.where(hit, jnp.int32(r), first)
        inv[2 * e] = first
        inv[2 * e + 1] = second

    loop(0, ne, place)
    lab_ext[0:ROWS, :] = lab_ref[...]
    lab_ext[ROWS:, :] = jnp.full((8, W), -1, I32)
    act[ROWS] = jnp.zeros((C, W), BF16)

    def put_labels(e):
        lab_snd[e, 0:1] = lab_ext[pl.ds(inv[2 * e], 1), :]
        lab_snd[e, 1:2] = lab_ext[pl.ds(inv[2 * e + 1], 1), :]

    loop(0, ne, put_labels)

    def lab_copy(at, e):
        return remote(lab_snd.at[e], lab_rcv.at[at], lab_s.at[0], lab_r.at[0], me_s, e)

    loop(1, ne, lambda k: lab_copy(me_e, epeer(k)).start())
    lab_rcv[pl.ds(me_e, 1)] = lab_snd[pl.ds(me_e, 1)]

    def drain_halo():
        for d, (ds, de) in enumerate(HALO):
            @pl.when(exists(ds, de))
            def _():
                halo_copy(d, me_s + ds, me_e + de).wait_send()

    drains.append(drain_halo)
    all_out(lab_snd.at[pl.ds(0, ne - 1)], lab_s.at[0])

    for load in loads[3:]:
        load.wait()

    for tap in range(27):
        a, b, c = tap // 9, tap // 3 % 3, tap % 3
        kwf[c * C:(c + 1) * C, (a * 3 + b) * C:(a * 3 + b + 1) * C] = k_ref[tap].astype(F32) * 0.5
    kw[...] = kwf[...].astype(BF16)
    w1 = w1_ref[...].astype(F32) * 0.5
    b1 = b1_ref[...].astype(F32) * 0.5
    w1full = jnp.concatenate([w1, b1, jnp.zeros((CLS - C - 1, HID), F32)], axis=0)
    w1t[...] = w1.astype(BF16)
    w1a[...] = w1full.T.astype(BF16)
    w2f[...] = jnp.zeros((CLS, HID), F32)
    w2f[0:NCLS, :] = w2_ref[...].astype(F32) * 0.5
    w2h[...] = w2f[...].astype(BF16)
    w2t[...] = w2f[...].T.astype(BF16)
    acc_c[0:8, :] = jnp.zeros((8, CLS), F32)
    acc_c[0:1, 0:NCLS] = b2_ref[...].astype(F32) * 0.5
    b2bc[...] = jnp.broadcast_to(acc_c[0:1, :], (CLS, CLS)).T

    classes = lax.broadcasted_iota(I32, (CLS, W), 0)
    lanes = lax.broadcasted_iota(I32, (C, W), 1)
    acc_i[...] = jnp.zeros((CLS, W), F32)
    acc_m[...] = jnp.zeros((CLS, W), F32)
    acc_c[...] = jnp.zeros((CLS, W), F32)
    acc_g[...] = jnp.zeros((CLS, W), F32)

    def count(r):
        acc_c[...] += jnp.where(classes == lab_ext[pl.ds(r, 1), :], 1.0, 0.0)

    loop(0, ROWS, count)
    x9[TAPS * C:, :] = jnp.zeros((96, ROWS * W), BF16)

    for d, (ds, de) in enumerate(HALO):
        @pl.when(exists(-ds, -de))
        def _():
            halo_copy(d, me_s - ds, me_e - de).wait_recv()

    def gather(z):
        for h in range(8):
            lane = slice((z * 8 + h) * W, (z * 8 + h + 1) * W)
            for a in range(3):
                x9[a * 96:(a + 1) * 96, lane] = xp[z + a, h:h + 3].reshape(96, W)

    for z in range(2):
        gather(z)

    def conv(p):
        lane = slice(p * BLK, (p + 1) * BLK)
        out = dot(kw[...], x9[0:TAPS * C, lane])
        for j in range(2):
            part = out[:, j * W:(j + 1) * W]
            left = jnp.where(lanes > 0, pltpu.roll(part[0:C], 1, 1), 0.0)
            right = jnp.where(lanes < W - 1, pltpu.roll(part[2 * C:3 * C], W - 1, 1), 0.0)
            v = left + part[C:2 * C] + right
            t = jnp.tanh(v)
            act[2 * p + j] = (v + v * t).astype(BF16)
            dconv[2 * p + j] = (1.0 + t) + v * (1.0 - t * t)

    for p in range(ROWS // 2):
        conv(p)

    def turn(i):
        m = i // 2 + 1
        return jnp.where(lax.rem(i, 2) == 0, m, ne - m)

    def row_copy(at, e):
        return remote(row_snd.at[e], row_rcv.at[at], row_s.at[0], row_r.at[at], me_s, e)

    def dispatch(i):
        e = epeer(turn(i))
        row_snd[e, 0] = act[inv[2 * e]]
        row_snd[e, 1] = act[inv[2 * e + 1]]
        row_copy(me_e, e).start()

    loop(0, ne - 1, dispatch)
    all_out(row_snd.at[pl.ds(0, ne - 1)], row_s.at[0])
    row_rcv[me_e, 0] = act[inv[2 * me_e]]
    row_rcv[me_e, 1] = act[inv[2 * me_e + 1]]

    ones = jnp.where(lax.broadcasted_iota(I32, (16, BLK), 0) == 0, 1.0, 0.0).astype(BF16)

    def forward(*blocks):
        xas, cols = [], []
        for s in blocks:
            col = pl.ds(pl.multiple_of(s * BLK, BLK), BLK)
            x = row_rcv[s]
            xa = jnp.concatenate([jnp.concatenate([x[0], x[1]], axis=1), ones], axis=0)
            xa_all[:, col] = xa
            xas.append(xa)
            cols.append(col)
        xa = jnp.concatenate(xas, axis=1)
        has = []
        for c in range(0, HID, 64):
            v = dot(w1a[c:c + 64, 0:48], xa)
            t = jnp.tanh(v)
            ha = (v + v * t).astype(BF16)
            d = (1.0 + t) + v * (1.0 - t * t)
            for n, col in enumerate(cols):
                ha_all[c:c + 64, col] = ha[:, n * BLK:(n + 1) * BLK]
                d_all[c:c + 64, col] = d[:, n * BLK:(n + 1) * BLK]
            has.append(ha)
        ha = jnp.concatenate(has, axis=0)
        for c in (0, 64):
            z = dot(w2h[c:c + 64, :], ha)
            for n, s in enumerate(blocks):
                lab = lab_rcv[s]
                for j in range(CAP):
                    lj = lab[j:j + 1, :]
                    at = n * BLK + j * W
                    t2 = jnp.tanh(z[:, at:at + W] + b2bc[c:c + 64, :])
                    t2 = jnp.where(lj < 0, 1.0, t2)
                    q_all[c:c + 64, pl.ds(pl.multiple_of(s * BLK + j * W, W), W)] = 1.0 - t2 * t2
                    acc_i[c:c + 64, :] += jnp.where(classes[c:c + 64] == lj, t2, 0.0)
                    acc_m[c:c + 64, :] += t2

    def arrived(s):
        row_copy(s, s).wait_recv()

    forward(me_e)

    def forward_turn(k):
        before, behind = epeer(ne - k), epeer(k)
        arrived(before)
        arrived(behind)
        forward(before, behind)

    all_in(lab_rcv.at[pl.ds(0, ne - 1)], lab_r.at[0])
    loop(1, half, forward_turn)
    arrived(epeer(half))
    forward(epeer(half))

    def lane_row(m):
        return jnp.sum(m.T, axis=0, keepdims=True)

    st1[pl.ds(me_e, 1)] = jnp.concatenate(
        [lane_row(acc_i[...]), lane_row(acc_m[...]), lane_row(acc_c[...]), jnp.zeros((1, CLS), F32)],
        axis=0,
    )[None]

    def st1_copy(e):
        return remote(st1.at[me_e], st1.at[me_e], st1_s.at[0], st1_r.at[0], me_s, e)

    each_e(lambda e: st1_copy(e).start())
    all_out(st1.at[pl.ds(0, ne - 1)], st1_s.at[0])
    all_in(st1.at[pl.ds(0, ne - 1)], st1_r.at[0])
    st2[pl.ds(me_s, 1)] = jnp.sum(st1[...], axis=0)[None]

    def st2_copy(s):
        return remote(st2.at[me_s], st2.at[me_s], st2_s.at[0], st2_r.at[0], s, me_e)

    each_s(lambda s: st2_copy(s).start())
    all_out(st2.at[pl.ds(0, ns - 1)], st2_s.at[0])
    all_in(st2.at[pl.ds(0, ns - 1)], st2_r.at[0])
    sums = jnp.sum(st2[...], axis=0)

    voxels = ns * ne * ROWS * W
    slots = ns * ne * ne * BLK
    scale = 16.0 * NCLS * math.sqrt(voxels)
    cnt = sums[2:3]
    inter = 0.5 * (cnt + sums[0:1])
    mass = 0.5 * sums[1:2] + (voxels - 0.5 * slots)
    denom = mass + cnt + 1.0
    dice = (2.0 * inter + 1.0) / denom
    real = lax.broadcasted_iota(I32, (1, CLS), 1) < NCLS
    loss_ref[...] = 1.0 - jnp.sum(jnp.where(real, dice, 0.0), axis=1, keepdims=True) / NCLS
    coef = jnp.where(real, (0.25 * scale / NCLS) / denom, 0.0)
    ab_b[...] = jnp.broadcast_to(coef * (dice - 2.0), (CLS, CLS)).T
    b_b[...] = jnp.broadcast_to(coef * dice, (CLS, CLS)).T

    def backward(dst, *blocks):
        tg = acc_g[...]
        gls, cols = [], []
        for s in blocks:
            col = pl.ds(pl.multiple_of(s * BLK, BLK), BLK)
            lab = lab_rcv[s]
            parts = []
            for j in range(CAP):
                eq = classes == lab[j:j + 1, :]
                g = jnp.where(eq, ab_b[...], b_b[...])
                g = g * q_all[:, pl.ds(pl.multiple_of(s * BLK + j * W, W), W)]
                tg = tg + g
                parts.append(g.astype(BF16))
            gl = jnp.concatenate(parts, axis=1)
            gl_all[:, col] = gl
            gls.append(gl)
            cols.append(col)
        gl = jnp.concatenate(gls, axis=1)
        ghs = []
        for c in range(0, HID, 64):
            g = dot(w2t[c:c + 64, :], gl)
            gh = jnp.concatenate(
                [(g[:, n * BLK:(n + 1) * BLK] * d_all[c:c + 64, col]).astype(BF16) for n, col in enumerate(cols)],
                axis=1,
            )
            for n, col in enumerate(cols):
                gh_all[c:c + 64, col] = gh[:, n * BLK:(n + 1) * BLK]
            ghs.append(gh)
        gx = dot(w1t[...], jnp.concatenate(ghs, axis=0)).astype(BF16)
        for n, s in enumerate(blocks):
            dst[s, 0] = gx[:, n * BLK:n * BLK + W]
            dst[s, 1] = gx[:, n * BLK + W:(n + 1) * BLK]
        acc_g[...] = tg

    def ret_copy(at, e):
        return remote(ret_snd.at[e], ret_rcv.at[at], ret_s.at[0], ret_r.at[0], me_s, e)

    def backward_turn(i):
        k = half - i
        before, behind = epeer(ne - k), epeer(k)
        backward(ret_snd, before, behind)
        ret_copy(me_e, before).start()
        ret_copy(me_e, behind).start()

    backward(ret_snd, epeer(half))
    ret_copy(me_e, epeer(half)).start()
    loop(1, half, backward_turn)
    all_out(ret_snd.at[pl.ds(0, ne - 1)], ret_s.at[0])
    backward(ret_rcv, me_e)

    all_in(ret_rcv.at[pl.ds(0, ne - 1)], ret_r.at[0])

    def conv_back(r):
        lane = slice(r * W, (r + 1) * W)
        e = ids_ref[r]
        j = jnp.where(inv[2 * e] == r, 0, 1)
        gp = (ret_rcv[e, j].astype(F32) * dconv[r]).astype(BF16).astype(F32)
        gp3[0:C, lane] = jnp.where(lanes < W - 1, pltpu.roll(gp, W - 1, 1), 0.0).astype(BF16)
        gp3[C:2 * C, lane] = gp.astype(BF16)
        gp3[2 * C:3 * C, lane] = jnp.where(lanes > 0, pltpu.roll(gp, 1, 1), 0.0).astype(BF16)

    for r in range(ROWS):
        conv_back(r)
    gkt = dot(gp3[...], x9[...], NT)
    tail = gkt[:, 256:]
    rest = tail[0:24]
    for g in range(1, 4):
        rest = rest + pltpu.roll(tail[24 * g:24 * g + 24], C * g, 1)
    full = jnp.concatenate([gkt[:, 0:128], gkt[:, 128:256], rest, jnp.zeros((40, CLS), F32)], axis=0)
    gka_snd[...] = full.astype(BF16).reshape(GROWS, 16, CLS)

    own = GROWS // ns

    def gka_copy(at, s):
        return remote(gka_snd.at[pl.ds(s * own, own)], gka_rcv.at[at], gka_s.at[0], gka_r.at[0], s, me_e)

    each_s(lambda s: gka_copy(me_s, s).start())
    all_out(gka_rcv.at[pl.ds(0, ns - 1)], gka_s.at[0])
    gka_rcv[pl.ds(me_s, 1)] = gka_snd[pl.ds(me_s * own, own)][None]
    egf[:, 0:8, :] = dot(gl_all[...], ha_all[...], NT).reshape(GROWS, 8, HID)
    gw1 = dot(xa_all[...], gh_all[...], NT)
    for i in range(GROWS):
        egf[i, 8:10, :] = gw1[2 * i:2 * i + 2, :]
        egf[i, 10:11, :] = gw1[C:C + 1, :]
        egf[i, 11:16, :] = jnp.zeros((5, HID), F32)
    gb2 = lane_row(acc_g[...])
    egf[0, 11:12, 0:CLS] = gb2
    eg_snd[...] = egf[...].astype(BF16)

    def eg_copy(at, s):
        return remote(eg_snd.at[pl.ds(s * own, own)], eg_rcv.at[at], eg_s.at[0], eg_r.at[0], s, me_e)

    loop(1, ns, lambda k: eg_copy(me_s, speer(k)).start())
    all_out(eg_rcv.at[pl.ds(0, ns - 1)], eg_s.at[0])
    eg_rcv[pl.ds(me_s, 1)] = eg_snd[pl.ds(me_s * own, own)][None]


    all_in(gka_rcv.at[pl.ds(0, ns - 1)], gka_r.at[0])
    gkb[pl.ds(me_e, 1)] = jnp.sum(gka_rcv[...].astype(F32), axis=0).astype(BF16)[None]

    def gkb_copy(e):
        return remote(gkb.at[me_e], gkb.at[me_e], gkb_s.at[0], gkb_r.at[0], me_s, e)

    each_e(lambda e: gkb_copy(e).start())
    all_out(gkb.at[pl.ds(0, ne - 1)], gkb_s.at[0])

    all_in(eg_rcv.at[pl.ds(0, ns - 1)], eg_r.at[0])
    eg_all[pl.ds(me_s * own, own)] = jnp.sum(eg_rcv[...].astype(F32), axis=0).astype(BF16)

    def ega_copy(s):
        part = eg_all.at[pl.ds(me_s * own, own)]
        return remote(part, part, ega_s.at[0], ega_r.at[0], s, me_e)

    loop(1, ns, lambda k: ega_copy(speer(k)).start())
    all_out(eg_all.at[pl.ds(0, (ns - 1) * own)], ega_s.at[0])

    all_in(gkb.at[pl.ds(0, ne - 1)], gkb_r.at[0])
    gkc[pl.ds(me_s * own, own)] = jnp.sum(gkb[...].astype(F32), axis=0).astype(BF16)

    def gkc_copy(s):
        part = gkc.at[pl.ds(me_s * own, own)]
        return remote(part, part, gkc_s.at[0], gkc_r.at[0], s, me_e)

    each_s(lambda s: gkc_copy(s).start())
    all_out(gkc.at[pl.ds(0, (ns - 1) * own)], gkc_s.at[0])
    all_in(eg_all.at[pl.ds(0, (ns - 1) * own)], ega_r.at[0])
    stores[0].start()
    stores[1].start()

    all_in(gkc.at[pl.ds(0, (ns - 1) * own)], gkc_r.at[0])
    stores[2].start()
    for drain in drains:
        drain()
    for store in stores:
        store.wait()


def write_out(
    loss_in, eg_in, gkc_in, loss_out, gk_out, gw1_out, gb1_out, gw2_out, gb2_out,
    loss, eg, gkc, gk, gw1, gb1, gw2, gb2, isem, osem,
):
    pairs = ((gkc_in, gkc), (eg_in, eg), (loss_in, loss))
    loads = [pltpu.make_async_copy(src, dst, isem.at[i]) for i, (src, dst) in enumerate(pairs)]
    for load in loads:
        load.start()
    loads[0].wait()
    full = gkc[...].astype(F32).reshape(GROWS * 16, CLS)
    rest = jnp.concatenate([full[192:216]] + [pltpu.roll(full[192:216], CLS - C * g, 1) for g in range(1, 4)], axis=0)
    for j in range(TAPS):
        turned = full[j // 4 * 96:j // 4 * 96 + 96] if j < 8 else rest
        if j % 4:
            turned = pltpu.roll(turned, CLS - C * (j % 4), 1)
        for c in range(3):
            gk[3 * j + c] = turned[c * C:(c + 1) * C, 0:C]
    pairs = ((gk, gk_out), (gw1, gw1_out), (gb1, gb1_out), (gw2, gw2_out.at[:, 0, :]), (gb2, gb2_out), (loss, loss_out))
    stores = [pltpu.make_async_copy(src, dst, osem.at[i]) for i, (src, dst) in enumerate(pairs)]
    stores[0].start()
    loads[1].wait()
    loads[2].wait()
    stores[5].start()
    final = eg[...].astype(F32)
    gw2[...] = final[:, 0:8, :].reshape(CLS, HID)[0:NCLS]
    stores[3].start()
    for i in range(GROWS):
        gw1[2 * i:2 * i + 2, :] = final[i, 8:10, :]
    gb1[...] = final[0, 10:11, :]
    gb2[...] = final[0, 11:12, 0:NCLS]
    for i in (1, 2, 4):
        stores[i].start()
    for store in stores:
        store.wait()


def on_device(
    features, kernel, labels, region_ids, first_weight, first_bias, second_weight, second_bias
):
    ns, ne = lax.axis_size("slab"), lax.axis_size("expert")
    cols = ne * BLK
    V = pltpu.VMEM
    own = GROWS // ns
    scratch = [
        V((C * ROWS, W), BF16),
        V((27, C, C), BF16),
        V((ROWS, W), I32),
        pltpu.SMEM((ROWS,), I32),
        V((C, HID), BF16),
        V((1, HID), BF16),
        V((NCLS, HID), BF16),
        V((1, NCLS), BF16),
        pltpu.SemaphoreType.DMA((8,)),
        V((1, 1), F32),
        pltpu.SemaphoreType.DMA((3,)),
        V((C * ROWS, W), F32),
        V((4, 10, C, W), BF16),
        V((3 * C, TAPS * C), F32),
        V((3 * C, TAPS * C), BF16),
        V((384, ROWS * W), BF16),
        V((ROWS + 1, C, W), BF16),
        V((ROWS, C, W), F32),
        V((ROWS + 8, W), I32),
        V((ne, CAP, W), I32),
        V((ne, CAP, W), I32),
        pltpu.SMEM((CAP * ne,), I32),
        V((HID, CLS), BF16),
        V((C, HID), BF16),
        V((CLS, HID), F32),
        V((CLS, HID), BF16),
        V((HID, CLS), BF16),
        V((CLS, W), F32),
        V((ne, CAP, C, W), BF16),
        V((ne, CAP, C, W), BF16),
        V((48, cols), BF16),
        V((HID, cols), BF16),
        V((HID, cols), F32),
        V((CLS, cols), F32),
        V((CLS, W), F32),
        V((CLS, W), F32),
        V((CLS, W), F32),
        V((ne, 4, CLS), F32),
        V((ns, 4, CLS), F32),
        V((CLS, W), F32),
        V((CLS, W), F32),
        V((CLS, cols), BF16),
        V((HID, cols), BF16),
        V((ne, CAP, C, W), BF16),
        V((ne, CAP, C, W), BF16),
        V((CLS, W), F32),
        V((GROWS, 16, HID), F32),
        V((GROWS, 16, HID), BF16),
        V((ns, own, 16, HID), BF16),
        V((GROWS, 16, HID), BF16),
        V((96, ROWS * W), BF16),
        V((GROWS, 16, CLS), BF16),
        V((ns, own, 16, CLS), BF16),
        V((ne, own, 16, CLS), BF16),
        V((GROWS, 16, CLS), BF16),
    ]
    sems = [8, 8, 1, 1, 1, ne] + [1] * 16
    scratch += [pltpu.SemaphoreType.DMA((n,)) for n in sems]
    hbm = pl.BlockSpec(memory_space=pltpu.HBM)
    outs = pl.pallas_call(
        functools.partial(body, ns, ne),
        out_shape=[
            jax.ShapeDtypeStruct((1, 1), F32),
            jax.ShapeDtypeStruct((GROWS, 16, HID), BF16),
            jax.ShapeDtypeStruct((GROWS, 16, CLS), BF16),
        ],
        in_specs=[hbm] * 8,
        out_specs=[hbm] * 3,
        scratch_shapes=scratch,
        compiler_params=pltpu.CompilerParams(
            collective_id=0, has_side_effects=True, vmem_limit_bytes=63 * 2**20
        ),
        name="fused_head",
    )(
        features.reshape(C * ROWS, W),
        kernel,
        labels.reshape(ROWS, W),
        region_ids.reshape(ROWS),
        jnp.swapaxes(first_weight, 1, 2).reshape(C, HID),
        first_bias,
        second_weight.reshape(NCLS, HID),
        second_bias,
    )
    loss, gk, gw1, gb1, gw2, gb2 = pl.pallas_call(
        write_out,
        out_shape=[
            jax.ShapeDtypeStruct((1, 1), F32),
            jax.ShapeDtypeStruct((27, C, C), F32),
            jax.ShapeDtypeStruct((C, HID), F32),
            jax.ShapeDtypeStruct((1, HID), F32),
            jax.ShapeDtypeStruct((NCLS, 1, HID), F32),
            jax.ShapeDtypeStruct((1, NCLS), F32),
        ],
        in_specs=[hbm] * 3,
        out_specs=[hbm] * 6,
        scratch_shapes=[
            V((1, 1), F32),
            V((GROWS, 16, HID), BF16),
            V((GROWS, 16, CLS), BF16),
            V((27, C, C), F32),
            V((C, HID), F32),
            V((1, HID), F32),
            V((NCLS, HID), F32),
            V((1, NCLS), F32),
            pltpu.SemaphoreType.DMA((3,)),
            pltpu.SemaphoreType.DMA((6,)),
        ],
        name="write_out",
    )(*outs)
    return (
        loss.reshape(()),
        gk,
        jnp.swapaxes(gw1.reshape(1, C, HID), 1, 2),
        gb1,
        jnp.swapaxes(gw2, 0, 1),
        gb2,
    )


def solution(mesh):
    in_specs = (
        P(None, "slab", "expert", None),
        P(),
        P("slab", "expert", None),
        P("slab", "expert", None, None),
        P("expert", None, None),
        P("expert", None),
        P("expert", None, None),
        P("expert", None),
    )
    out_specs = (
        P(),
        P(),
        P("expert", None, None),
        P("expert", None),
        P("expert", None, None),
        P("expert", None),
    )
    return jax.shard_map(
        on_device, mesh=mesh, in_specs=in_specs, out_specs=out_specs, check_vma=False
    )
```
